32 devices in a mesh: tok: 16 (over z, y, x), ch: 2 (over core).
Axes of the slice: x: 2, y: 2, z: 4, core: 2. Of those that a mesh axis runs over, the one named last changes fastest.
Arguments:
- hidden: bfloat16 [2048, 1024], P('tok'), may hold values from -13 to 13
- pre_gates: bfloat16 [2, 2048, 1024], P(None, 'tok', 'ch'), may hold values from -6 to 6
- conv_weight: bfloat16 [2, 4, 1024, 1024], P(None, None, 'tok', 'ch'), may hold values from -0.09375 to 0.09375
- head_weight: bfloat16 [1024, 20480], P('tok', 'ch'), may hold values from -8 to 8
- cluster_weight: bfloat16 [1024, 32], P('tok', 'ch'), may hold values from -0.59765625 to 0.59765625
- tail1_proj: bfloat16 [16, 1024, 256], P('tok'), may hold values from -1 to 1
- tail2_proj: bfloat16 [16, 1024, 64], P('tok'), may hold values from -1 to 1
- tail1_out: bfloat16 [16, 256, 3072], P('tok', None, 'ch'), may hold values from -12 to 12
- tail2_out: bfloat16 [16, 64, 9216], P('tok', None, 'ch'), may hold values from -30 to 30
- cluster_id: int32 [2048], P('tok'), may hold values from -1 to 31, as said below
- target: int32 [2048], P('tok'), may hold values from 0 to 20479, as said below
Outputs:
- token_loss: float32 [2048], P('tok')
- grad_input: bfloat16 [2048, 1024], P('tok', 'ch')
- proj1_grad: float32 [16, 1024, 256], P('tok', 'ch')
- proj2_grad: float32 [16, 1024, 64], P('tok', 'ch')
- out1_grad: float32 [16, 256, 3072], P('tok', None, 'ch')
- out2_grad: float32 [16, 64, 9216], P('tok', None, 'ch')
The draws below stay inside these ranges and needn't reach their ends.
Inputs may be any that keep to these rules, and one draw needn't show every extreme that they name: `cluster_id`: in each aligned block of 128 tokens at most 8 name clusters of one owner; in every draw one owner is named by 8 tokens of every block, and every owner by 8 tokens of some block. `target`: below 20480 for a head token, below 3072 for a first-tier token, below 9216 for a second-tier token.
All inputs are finite; a program needn't handle non-finite values.
Results may differ from the reference program's by a relative error of at most 0.01.
Values may be sent and summed in bfloat16 or wider, within the bound.
A program may use at most 128 MiB of HBM per device.

```python
import math
import jax
import jax.numpy as jnp
from jax import lax

D = 1024
HEAD = 20480
P1 = 256
P2 = 64
W1 = 3072
W2 = 9216
K = 4
LEN = 128
TOK_DEV = 128
OWNERS = 16
TOKENS = 2048
CAP = 8
SLOTS = 128
CLUST = 32
N_TOK = 16
N_CH = 2


def routing(key):
    key_list = jax.random.split(jax.random.fold_in(key, 101), 6)
    full_owner = jax.random.randint(key_list[0], (), 0, OWNERS)
    shift_owner = jax.random.randint(key_list[1], (), 0, OWNERS)
    blocks = jnp.arange(OWNERS, dtype=jnp.int32)
    chosen = (blocks + shift_owner) % OWNERS
    orders = jax.vmap(lambda block_key: jax.random.permutation(block_key, TOK_DEV))(jax.random.split(key_list[2], OWNERS)).astype(jnp.int32)
    position = jnp.arange(TOK_DEV, dtype=jnp.int32)[None, :]
    forced_full = jnp.broadcast_to(position < CAP, (OWNERS, TOK_DEV))
    forced_own = (position >= CAP) & (position < 2 * CAP) & (chosen[:, None] != full_owner)
    random_tail = jax.random.randint(key_list[3], (OWNERS, TOK_DEV), 0, 2) == 1
    random_owner = jax.random.randint(key_list[4], (OWNERS, TOK_DEV), 0, OWNERS)
    random_tier = jax.random.randint(key_list[5], (OWNERS, TOK_DEV), 0, 2)
    owner_ids = jnp.where(forced_full, full_owner, jnp.where(forced_own, chosen[:, None], random_owner))
    tier_ids = jnp.where(forced_full | forced_own, position % 2, random_tier)
    wanted = forced_full | forced_own | random_tail
    hits = ((owner_ids[:, :, None] == blocks[None, None, :]) & wanted[:, :, None]).astype(jnp.int32)
    running = jnp.cumsum(hits, axis=1)
    rank = jnp.sum(running * hits, axis=2) - 1
    kept = wanted & (rank < CAP)
    cluster_order = jnp.where(kept, 2 * owner_ids + tier_ids, -1).astype(jnp.int32)
    row_index = blocks[:, None]
    cluster = jnp.zeros((OWNERS, TOK_DEV), jnp.int32).at[row_index, orders].set(cluster_order)
    return (cluster.reshape(TOKENS), orders, full_owner, shift_owner)


def aligned(key):
    cluster, orders, full_owner, shift_owner = routing(key)
    owner_range = jnp.arange(OWNERS, dtype=jnp.int32)
    is_full = owner_range == full_owner
    block = jnp.where(is_full, 0, (owner_range - shift_owner) % OWNERS)
    parity = CAP % 2
    first_pos = jnp.where(is_full, 0, CAP + parity)
    second_pos = jnp.where(is_full, 1, CAP + 1 - parity)
    first_tok = block * TOK_DEV + orders[block, first_pos]
    second_tok = block * TOK_DEV + orders[block, second_pos]
    head_tok = jax.random.randint(jax.random.fold_in(key, 303), (8,), 0, TOKENS)
    return (first_tok, second_tok, head_tok)


def hidden_rows(key):
    key_list = jax.random.split(jax.random.fold_in(key, 404), 3)
    first_tok, second_tok, head_tok = aligned(key)
    base_draw = jnp.clip(jax.random.normal(key_list[0], (TOKENS, D)), -6.0, 6.0)
    row_scale = jnp.exp(jax.random.uniform(key_list[2], (TOKENS, 1), minval=math.log(0.5), maxval=math.log(2.0)))
    marked = jnp.zeros((TOKENS,), jnp.int32).at[jnp.concatenate([first_tok, second_tok, head_tok])].set(1)
    row_scale = jnp.where(marked[:, None] == 1, 1.0, row_scale)
    return base_draw * row_scale


def draw_hidden(key, part):
    return hidden_rows(key).astype(jnp.bfloat16)


def draw_head_weight(key, part):
    key_list = jax.random.split(jax.random.fold_in(key, 505), 2)
    columns = jnp.arange(HEAD, dtype=jnp.float32) / HEAD
    base_draw = jnp.clip(jax.random.normal(key_list[0], (D, HEAD)), -6.0, 6.0)
    col_power = 0.5 * columns + 0.5 * jax.random.uniform(key_list[1], (HEAD,))
    weight = base_draw * jnp.power(10.0, col_power)[None, :] / math.sqrt(D)
    return weight.astype(jnp.bfloat16)


def tail_proj(key, which, proj_width):
    base_key = jax.random.fold_in(key, 606 + which)
    base_draw = jnp.clip(jax.random.normal(base_key, (OWNERS, D, proj_width)), -6.0, 6.0)
    return base_draw / math.sqrt(D)


def tail_out(key, which, proj_width, word_count):
    key_list = jax.random.split(jax.random.fold_in(key, 707 + which), 2)
    columns = jnp.arange(word_count, dtype=jnp.float32) / word_count
    base_draw = jnp.clip(jax.random.normal(key_list[0], (OWNERS, proj_width, word_count)), -6.0, 6.0)
    col_power = 0.5 * columns + 0.5 * jax.random.uniform(key_list[1], (OWNERS, 1, word_count))
    weight = base_draw * jnp.power(10.0, col_power) / math.sqrt(proj_width)
    return weight


def draw_tail1_proj(key, part):
    return tail_proj(key, 0, P1).astype(jnp.bfloat16)


def draw_tail2_proj(key, part):
    return tail_proj(key, 1, P2).astype(jnp.bfloat16)


def draw_tail1_out(key, part):
    return tail_out(key, 0, P1, W1).astype(jnp.bfloat16)


def draw_tail2_out(key, part):
    return tail_out(key, 1, P2, W2).astype(jnp.bfloat16)


def draw_cluster_id(key, part):
    return routing(key)[0]


def draw_target(key, part):
    cluster = routing(key)[0]
    key_list = jax.random.split(jax.random.fold_in(key, 202), 3)
    head_word = jax.random.randint(key_list[0], (TOKENS,), 0, HEAD)
    first_word = jax.random.randint(key_list[1], (TOKENS,), 0, W1)
    second_word = jax.random.randint(key_list[2], (TOKENS,), 0, W2)
    words = jnp.where(cluster < 0, head_word, jnp.where(cluster % 2 == 0, first_word, second_word)).astype(jnp.int32)
    first_head = jnp.argmax((cluster < 0).astype(jnp.int32)).astype(jnp.int32)
    return words.at[first_head].set(HEAD - 1).astype(jnp.int32)


def shard_levels(own_key, dims, cuts, low, high):
    loudness, own = 1.0, jax.random.fold_in(own_key, 6)
    for axis_at, blocks in cuts:
        draws = jnp.exp(jax.random.uniform(jax.random.fold_in(own, axis_at), (blocks,), jnp.float32, low / len(cuts), high / len(cuts)))
        loudness = loudness * jnp.repeat(draws, dims[axis_at] // blocks).reshape([-1 if axis == axis_at else 1 for axis in range(len(dims))])
    return loudness


def scatter_about(key, dims, scale, reach, cuts=(), kind=jnp.bfloat16):
    entries = jax.random.normal(key, dims, jnp.float32) * scale
    if len(cuts) > 0:
        entries = shard_levels(key, dims, cuts, -0.22, 0.18) * entries
    return jnp.clip(entries, min=-reach, max=reach).astype(kind)


def setup_inputs(seed: int = 0) -> dict:
    arg_keys = jax.random.split(jax.random.key(seed), 12)
    hidden = draw_hidden(jax.random.fold_in(arg_keys[11], 71), 0)
    pre_gates = scatter_about(arg_keys[1], (2, TOKENS, D), 1.0, 6.0, ((1, 16), (2, 2)))
    conv_weight = scatter_about(arg_keys[2], (2, K, D, D), (K * D) ** -0.5, 0.09375, ((2, 16), (3, 2)))
    head_weight = draw_head_weight(jax.random.fold_in(arg_keys[11], 71), 0)
    cluster_weight = scatter_about(arg_keys[4], (D, CLUST), 0.1, 0.59765625, ((0, 16), (1, 2)))
    tail1_proj = draw_tail1_proj(jax.random.fold_in(arg_keys[11], 71), 0)
    tail2_proj = draw_tail2_proj(jax.random.fold_in(arg_keys[11], 71), 0)
    tail1_out = draw_tail1_out(jax.random.fold_in(arg_keys[11], 71), 0)
    tail2_out = draw_tail2_out(jax.random.fold_in(arg_keys[11], 71), 0)
    cluster_id = draw_cluster_id(jax.random.fold_in(arg_keys[11], 71), 0)
    target = draw_target(jax.random.fold_in(arg_keys[11], 71), 0)
    return {"hidden": hidden, "pre_gates": pre_gates, "conv_weight": conv_weight, "head_weight": head_weight, "cluster_weight": cluster_weight, "tail1_proj": tail1_proj, "tail2_proj": tail2_proj, "tail1_out": tail1_out, "tail2_out": tail2_out, "cluster_id": cluster_id, "target": target}


def rounded(values):
    return lax.optimization_barrier(values.astype(jnp.bfloat16))


def merge_groups(row_max, row_sum, row_value):
    merged_max = jnp.max(row_max, axis=1)
    factor = jnp.exp(row_max - merged_max[:, None])
    merged_sum = jnp.sum(row_sum * factor, axis=1)
    merged_value = jnp.sum(row_value * factor[:, :, None], axis=1)
    return merged_max + jnp.log(merged_sum), merged_value / merged_sum[:, None]


def head_block(row_block, word_ids, cluster_ids, head_weight, cluster_weight, grouped_weight):
    row_count = row_block.shape[0]
    word_logits = jnp.dot(row_block, head_weight, preferred_element_type=jnp.float32).reshape(row_count, N_CH, -1)
    cluster_logits = jnp.dot(row_block, cluster_weight, preferred_element_type=jnp.float32).reshape(row_count, N_CH, -1)
    logits = jnp.concatenate([word_logits, cluster_logits], axis=2)
    row_max = jnp.max(logits, axis=2)
    expo_terms = jnp.exp(logits - row_max[:, :, None])
    row_sum = jnp.sum(expo_terms, axis=2)
    weights = rounded(expo_terms).astype(jnp.float32)
    row_value = jnp.einsum("bgj,dgj->bgd", weights, grouped_weight)
    log_total, mean_value = merge_groups(row_max, row_sum, row_value)
    head_words = HEAD // N_CH
    group_size = CLUST // N_CH
    is_tail = cluster_ids >= 0
    safe_cluster = jnp.maximum(cluster_ids, 0)
    group_index = jnp.where(is_tail, safe_cluster // group_size, word_ids // head_words).astype(jnp.int32)
    inner_index = jnp.where(is_tail, head_words + safe_cluster % group_size, word_ids % head_words).astype(jnp.int32)
    picked = logits[jnp.arange(row_count, dtype=jnp.int32), group_index, inner_index]
    column_value = grouped_weight[:, group_index, inner_index].T
    return log_total - picked, mean_value - column_value


def tier_terms(rows, word_ids, member, proj, out):
    features = rounded(jnp.dot(rows, proj, preferred_element_type=jnp.float32))
    logits = jnp.dot(features, out, preferred_element_type=jnp.float32)
    row_count = logits.shape[0]
    grouped = logits.reshape(row_count, N_CH, -1)
    row_max = jnp.max(grouped, axis=2)
    expo_terms = jnp.exp(grouped - row_max[:, :, None])
    row_sum = jnp.sum(expo_terms, axis=2)
    weights = rounded(expo_terms).astype(jnp.float32)
    out_grouped = out.reshape(out.shape[0], N_CH, -1).astype(jnp.float32)
    row_value = jnp.einsum("sgj,pgj->sgp", weights, out_grouped)
    log_total, mean_value = merge_groups(row_max, row_sum, row_value)
    column = jnp.clip(word_ids, 0, out.shape[1] - 1).astype(jnp.int32)
    picked = jnp.take_along_axis(logits, column[:, None], axis=1)[:, 0]
    column_value = jnp.take(out, column, axis=1).T.astype(jnp.float32)
    tail_dz = rounded(jnp.where(member[:, None], mean_value - column_value, 0.0))
    probability = jnp.exp(logits - log_total[:, None])
    positions = jnp.arange(out.shape[1], dtype=jnp.int32)
    target_hot = (positions[None, :] == column[:, None]).astype(jnp.float32)
    dlogit = rounded(jnp.where(member[:, None], probability - target_hot, 0.0))
    out_grad = jnp.einsum("sp,sw->pw", features.astype(jnp.float32), dlogit.astype(jnp.float32))
    proj_grad = jnp.einsum("sd,sp->dp", rows.astype(jnp.float32), tail_dz.astype(jnp.float32))
    returned = jnp.einsum("sp,dp->sd", tail_dz.astype(jnp.float32), proj.astype(jnp.float32))
    tail_loss = jnp.where(member, log_total - picked, 0.0)
    return out_grad, proj_grad, returned, tail_loss


def reference(hidden, pre_gates, conv_weight, head_weight, cluster_weight, tail1_proj, tail2_proj, tail1_out, tail2_out, cluster_id, target):
    grouped_weight = jnp.concatenate([head_weight.reshape(D, N_CH, -1), cluster_weight.reshape(D, N_CH, -1)], axis=2).astype(jnp.float32)

    def head_step(pieces):
        return head_block(pieces[0], pieces[1], pieces[2], head_weight, cluster_weight, grouped_weight)

    head_loss, head_grad = lax.map(head_step, (hidden.reshape(N_TOK, TOK_DEV, D), target.reshape(N_TOK, TOK_DEV), cluster_id.reshape(N_TOK, TOK_DEV)))
    head_loss = head_loss.reshape(TOKENS)
    head_grad = head_grad.reshape(TOKENS, D)

    tokens_all = jnp.arange(TOKENS, dtype=jnp.int32)
    is_tail = cluster_id >= 0
    owner_ids = jnp.where(is_tail, cluster_id // 2, 0).astype(jnp.int32)
    tier_ids = jnp.where(is_tail, cluster_id % 2, -1).astype(jnp.int32)
    source = tokens_all // TOK_DEV
    owner_range = jnp.arange(OWNERS, dtype=jnp.int32)
    hits = ((owner_ids.reshape(N_TOK, TOK_DEV, 1) == owner_range[None, None, :]) & is_tail.reshape(N_TOK, TOK_DEV, 1)).astype(jnp.int32)
    running = jnp.cumsum(hits, axis=1)
    slot_ids = (jnp.sum(running * hits, axis=2) - 1).reshape(TOKENS).astype(jnp.int32)
    flat_index = jnp.where(is_tail, owner_ids * SLOTS + source * CAP + slot_ids, OWNERS * SLOTS).astype(jnp.int32)
    table = jnp.full((OWNERS * SLOTS + 1,), TOKENS, jnp.int32).at[flat_index].set(tokens_all)[:-1].reshape(OWNERS, SLOTS)
    hidden_pad = jnp.concatenate([hidden, jnp.zeros((1, D), jnp.bfloat16)], axis=0)
    target_pad = jnp.concatenate([target, jnp.zeros((1,), jnp.int32)], axis=0)
    tier_pad = jnp.concatenate([tier_ids, jnp.full((1,), -1, jnp.int32)], axis=0)

    def owner_step(pieces):
        index_row, first_proj, second_proj, first_out, second_out = pieces
        rows = hidden_pad[index_row]
        word_ids = target_pad[index_row]
        tiers = tier_pad[index_row]
        first = tier_terms(rows, word_ids, tiers == 0, first_proj, first_out)
        second = tier_terms(rows, word_ids, tiers == 1, second_proj, second_out)
        return first[0], second[0], first[1], second[1], first[2] + second[2], first[3] + second[3]

    out1_grad, out2_grad, proj1_grad, proj2_grad, returned, tail_loss = lax.map(owner_step, (table, tail1_proj, tail2_proj, tail1_out, tail2_out))
    table_flat = table.reshape(-1)
    tail_back = jnp.zeros((TOKENS + 1, D), jnp.float32).at[table_flat].set(returned.reshape(-1, D))[:TOKENS]
    tail_tok_loss = jnp.zeros((TOKENS + 1,), jnp.float32).at[table_flat].set(tail_loss.reshape(-1))[:TOKENS]
    token_loss = head_loss + tail_tok_loss

    grad_sum = head_grad + tail_back
    gate_a = pre_gates[0].astype(jnp.float32)
    gate_sig = jax.nn.sigmoid(pre_gates[1].astype(jnp.float32))
    grad_a = (grad_sum * gate_sig).astype(jnp.bfloat16)
    grad_b = (grad_sum * gate_a * gate_sig * (1.0 - gate_sig)).astype(jnp.bfloat16)
    total_grad = grad_sum
    for offset_rows in range(K):
        for half_index, gate_grad in ((0, grad_a), (1, grad_b)):
            blocks = gate_grad.reshape(TOKENS // LEN, LEN, D)
            shifted = jnp.pad(blocks[:, offset_rows:], ((0, 0), (0, offset_rows), (0, 0))).reshape(TOKENS, D)
            total_grad = total_grad + jnp.dot(shifted, conv_weight[half_index, offset_rows].T, preferred_element_type=jnp.float32)
    grad_input = total_grad.astype(jnp.bfloat16)
    return (token_loss, grad_input, proj1_grad, proj2_grad, out1_grad, out2_grad)
```

```python
import jax
import jax.numpy as jnp
from jax import lax
from jax.sharding import Mesh, PartitionSpec as P

K = 4
LEN = 128
LANES = 128
TOK = ("hi", "lo")
BF = jnp.bfloat16
F32 = jnp.float32


def dot(a, b):
    return jnp.dot(a, b, preferred_element_type=F32)


def dot_t(a, b):
    return lax.dot_general(a, b, (((1,), (1,)), ((), ())), preferred_element_type=F32)


def t_dot(a, b):
    return lax.dot_general(a, b, (((0,), (0,)), ((), ())), preferred_element_type=F32)


def merge_stats(stats):
    top = jnp.max(stats[:, 0], axis=0)
    total = jnp.sum(stats[:, 1] * jnp.exp(stats[:, 0] - top), axis=0)
    return top, total


def running_count(mine):
    local = mine.shape[1]
    upto = (jnp.arange(local)[:, None] <= jnp.arange(local)[None, :]).astype(F32)
    within = dot(mine, upto)
    blocks = mine.shape[0]
    before = (jnp.arange(blocks)[None, :] < jnp.arange(blocks)[:, None]).astype(F32)
    return within + dot(before, within[:, -1:])


def tier_start(rows, word_ids, proj, out_shard, ch_index):
    features = dot(rows, proj).astype(BF)
    logits = dot(features, out_shard)
    top = jnp.max(logits, axis=1)
    total = jnp.sum(jnp.exp(logits - top[:, None]), axis=1)
    width = out_shard.shape[1]
    positions = jnp.arange(width, dtype=jnp.int32) + ch_index * width
    hot = positions[None, :] == word_ids[:, None]
    picked = jnp.sum(jnp.where(hot, logits, 0.0), axis=1)
    return features, logits, hot, picked, jnp.stack([top, total])


def tier_slope(logits, hot, member, log_total):
    slope = jnp.exp(logits - log_total[:, None]) - hot.astype(F32)
    return jnp.where(member[:, None], slope, 0.0).astype(BF)


def on_device(
    hidden,
    pre_gates,
    conv_weight,
    head_weight,
    cluster_weight,
    tail1_proj,
    tail2_proj,
    tail1_out,
    tail2_out,
    cluster_id,
    target,
):
    local, model_width = hidden.shape
    owners = lax.axis_size(TOK)
    groups = lax.axis_size("ch")
    lo = lax.axis_size("lo")
    me = lax.axis_index(TOK)
    ch_index = lax.axis_index("ch")
    tokens = local * owners
    slots = max(2, local // owners) * owners
    narrow = model_width // groups
    col_start = ch_index * narrow

    hidden_part = lax.dynamic_slice_in_dim(hidden, col_start, narrow, 1)
    hidden_cols = lax.all_gather(hidden_part, TOK, axis=0, tiled=True)
    hidden_all = lax.all_gather(hidden_cols, "ch", axis=1, tiled=True)
    meta = lax.all_gather(jnp.stack([cluster_id, target]), TOK, axis=1, tiled=True)
    cluster_all, target_all = meta[0], meta[1]

    words = head_weight.shape[1] // owners
    clusters = cluster_weight.shape[1]
    word_part = lax.all_to_all(head_weight, TOK, split_axis=1, concat_axis=0, tiled=True)
    cluster_part = lax.all_gather(cluster_weight, TOK, axis=0, tiled=True)
    conv_part = lax.all_gather(conv_weight, "hi", axis=2, tiled=True)

    mine = (cluster_all >= 0) & (cluster_all // 2 == me)
    rank = running_count(mine.reshape(owners, local).astype(F32)).reshape(tokens)
    slot_ids = jnp.where(mine, rank.astype(jnp.int32) - 1, -1)
    chosen = slot_ids[:, None] == jnp.arange(slots, dtype=jnp.int32)[None, :]
    chosen_bf = chosen.astype(BF)
    rows = t_dot(chosen_bf, hidden_all).astype(BF)
    word_ids = jnp.sum(jnp.where(chosen, target_all[:, None], 0), axis=0)
    tiers = jnp.sum(jnp.where(chosen, cluster_all[:, None] % 2 + 1, 0), axis=0)
    first_member, second_member = tiers == 1, tiers == 2
    first_proj, second_proj = tail1_proj[0], tail2_proj[0]
    first_out, second_out = tail1_out[0], tail2_out[0]
    first_features, first_logits, first_hot, first_pick, first_stats = tier_start(
        rows, word_ids, first_proj, first_out, ch_index
    )
    second_features, second_logits, second_hot, second_pick, second_stats = tier_start(
        rows, word_ids, second_proj, second_out, ch_index
    )
    stats = lax.all_gather(jnp.stack([first_stats, second_stats], axis=1), "ch")
    top, total = merge_stats(stats)
    tail_log = top + jnp.log(total)
    first_slope = tier_slope(first_logits, first_hot, first_member, tail_log[0])
    second_slope = tier_slope(second_logits, second_hot, second_member, tail_log[1])
    dz = jnp.concatenate(
        [dot_t(first_slope, first_out), dot_t(second_slope, second_out)], axis=1
    )
    dz = jnp.sum(lax.all_gather(dz, "ch"), axis=0).astype(BF)
    first_dz = dz[:, : first_proj.shape[1]]
    second_dz = dz[:, first_proj.shape[1] :]
    back = dot_t(first_dz, first_proj) + dot_t(second_dz, second_proj)
    col_group = jnp.arange(model_width, dtype=jnp.int32)[None, :] // narrow
    back = jnp.where(col_group == ch_index, back, 0.0).astype(BF)
    once = jnp.where(ch_index == 0, 1.0, 0.0)
    tail_loss = jnp.where(first_member, once * tail_log[0] - first_pick, 0.0)
    tail_loss = tail_loss + jnp.where(second_member, once * tail_log[1] - second_pick, 0.0)
    first_out_grad = t_dot(first_features, first_slope)
    second_out_grad = t_dot(second_features, second_slope)
    rows_part = lax.dynamic_slice_in_dim(rows, col_start, narrow, 1)
    first_proj_grad = t_dot(rows_part, first_dz)
    second_proj_grad = t_dot(rows_part, second_dz)

    spare = -(words + clusters) % LANES
    columns = jnp.concatenate(
        [word_part, cluster_part, jnp.zeros((model_width, spare), BF)], axis=1
    )
    place = jnp.arange(columns.shape[1], dtype=jnp.int32)[None, :]
    limit = jnp.where(me == 0, words + clusters, words)
    logits = jnp.where(place < limit, dot(hidden_all, columns), -jnp.inf)
    top = jnp.max(logits, axis=1)
    total = jnp.sum(jnp.exp(logits - top[:, None]), axis=1)
    is_tail = cluster_all >= 0
    word_place = target_all - (ch_index * owners + me) * words
    word_place = jnp.where((word_place >= 0) & (word_place < words), word_place, -1)
    cluster_place = cluster_all - ch_index * clusters
    cluster_here = (cluster_place >= 0) & (cluster_place < clusters) & (me == 0)
    cluster_place = jnp.where(cluster_here, cluster_place + words, -1)
    hot = place == jnp.where(is_tail, cluster_place, word_place)[:, None]
    picked = jnp.sum(jnp.where(hot, logits, 0.0), axis=1)
    stats = lax.all_gather(jnp.stack([top, total]), "ch")
    stats = lax.all_gather(jnp.stack(merge_stats(stats)), TOK)
    top, total = merge_stats(stats)
    head_log = top + jnp.log(total)
    slope = (jnp.exp(logits - head_log[:, None]) - hot.astype(F32)).astype(BF)
    grad_part = dot_t(
        jnp.concatenate([slope, chosen_bf], axis=1),
        jnp.concatenate([columns, back.T], axis=1),
    ).astype(BF)
    grad_cols = lax.psum_scatter(grad_part, "ch", scatter_dimension=1, tiled=True)
    grad_sum = lax.psum_scatter(grad_cols, TOK, scatter_dimension=0, tiled=True).astype(F32)

    loss_part = jnp.sum(jnp.where(chosen, tail_loss[None, :], 0.0), axis=1) - picked
    loss_part = jnp.sum(lax.all_gather(loss_part, "ch"), axis=0)
    own_loss = lax.psum_scatter(loss_part, TOK, scatter_dimension=0, tiled=True)
    token_loss = own_loss + lax.dynamic_slice_in_dim(head_log, me * local, local, 0)

    gate_a = pre_gates[0].astype(F32)
    gate_sig = jax.nn.sigmoid(pre_gates[1].astype(F32))
    gate_grads = jnp.stack(
        [grad_sum * gate_sig, grad_sum * gate_a * gate_sig * (1.0 - gate_sig)]
    ).astype(BF)
    gates = lax.all_gather(gate_grads, "lo", axis=1, tiled=True)
    near = gates.shape[1]
    blocks = gates.reshape(2, near // LEN, LEN, narrow)
    shifted = jnp.stack(
        [
            jnp.pad(blocks[:, :, offset:], ((0, 0), (0, 0), (0, offset), (0, 0))).reshape(
                2, near, narrow
            )
            for offset in range(K)
        ]
    )
    conv_terms = jnp.einsum(
        "kgtc,gkrc->tr", shifted, conv_part, preferred_element_type=F32
    ).astype(BF)
    conv_terms = lax.all_to_all(
        conv_terms.reshape(lo, local, -1), "lo", split_axis=0, concat_axis=0, tiled=True
    )
    share = conv_weight.shape[2]
    conv_terms = conv_terms.reshape(lo, local, -1, share).transpose(1, 2, 0, 3)
    conv_grad = lax.psum_scatter(
        conv_terms.reshape(local, model_width), "ch", scatter_dimension=1, tiled=True
    )
    grad_input = (grad_sum + conv_grad.astype(F32)).astype(BF)
    return (
        token_loss,
        grad_input,
        first_proj_grad[None],
        second_proj_grad[None],
        first_out_grad[None],
        second_out_grad[None],
    )


def solution(mesh):
    n_tok, n_ch = mesh.shape["tok"], mesh.shape["ch"]
    lo = 1
    while n_tok % (lo * 2) == 0 and lo * lo * 4 <= n_tok:
        lo *= 2
    split = Mesh(mesh.devices.reshape(n_tok // lo, lo, n_ch), ("hi", "lo", "ch"))
    placed = (
        P(TOK, None),
        P(None, TOK, "ch"),
        P(None, None, TOK, "ch"),
        P(TOK, "ch"),
        P(TOK, "ch"),
        P(TOK, None, None),
        P(TOK, None, None),
        P(TOK, None, "ch"),
        P(TOK, None, "ch"),
        P(TOK),
        P(TOK),
    )
    return jax.shard_map(
        on_device,
        mesh=split,
        in_specs=placed,
        out_specs=(
            P(TOK),
            P(TOK, "ch"),
            P(TOK, "ch", None),
            P(TOK, "ch", None),
            P(TOK, None, "ch"),
            P(TOK, None, "ch"),
        ),
        check_vma=False,
    )
```

```python
import jax
import jax.numpy as jnp
from jax import lax
from jax.sharding import Mesh, PartitionSpec as P

LEN = 128
LANES = 128
TOK = ("hi", "lo")
BF = jnp.bfloat16
F32 = jnp.float32


def dot(a, b):
    return jnp.dot(a, b, preferred_element_type=F32)


def dot_t(a, b):
    return lax.dot_general(a, b, (((1,), (1,)), ((), ())), preferred_element_type=F32)


def t_dot(a, b):
    return lax.dot_general(a, b, (((0,), (0,)), ((), ())), preferred_element_type=F32)


def merge_stats(stats):
    top = jnp.max(stats[:, 0], axis=0)
    total = jnp.sum(stats[:, 1] * jnp.exp(stats[:, 0] - top), axis=0)
    return top, total


def exchange(x, axis):
    return lax.all_to_all(x, axis, split_axis=0, concat_axis=0, tiled=True)


def spread(x, axis):
    return exchange(jnp.broadcast_to(x[None], (lax.axis_size(axis), *x.shape)), axis)


def turned(x, step):
    groups = lax.axis_size("ch")
    return lax.ppermute(x, "ch", [(k, (k + step) % groups) for k in range(groups)])


def running_count(mine):
    local = mine.shape[1]
    upto = (jnp.arange(local)[:, None] <= jnp.arange(local)[None, :]).astype(F32)
    within = dot(mine, upto)
    blocks = mine.shape[0]
    before = (jnp.arange(blocks)[None, :] < jnp.arange(blocks)[:, None]).astype(F32)
    return within + dot(before, within[:, -1:])


def tier_start(rows, word_ids, proj, out_shard, ch_index):
    features = dot(rows, proj).astype(BF)
    logits = dot(features, out_shard)
    top = jnp.max(logits, axis=1)
    total = jnp.sum(jnp.exp(logits - top[:, None]), axis=1)
    width = out_shard.shape[1]
    positions = jnp.arange(width, dtype=jnp.int32) + ch_index * width
    hot = positions[None, :] == word_ids[:, None]
    picked = jnp.sum(jnp.where(hot, logits, 0.0), axis=1)
    return features, logits, hot, picked, jnp.stack([top, total])


def tier_slope(logits, hot, member, log_total):
    slope = jnp.exp(logits - log_total[:, None]) - hot.astype(F32)
    return jnp.where(member[:, None], slope, 0.0).astype(BF)


def on_device(
    hidden,
    pre_gates,
    conv_weight,
    head_weight,
    cluster_weight,
    tail1_proj,
    tail2_proj,
    tail1_out,
    tail2_out,
    cluster_id,
    target,
):
    local, model_width = hidden.shape
    owners = lax.axis_size(TOK)
    groups = lax.axis_size("ch")
    lo = lax.axis_size("lo")
    me = lax.axis_index(TOK)
    ch_index = lax.axis_index("ch")
    tokens = local * owners
    slots = max(2, local // owners) * owners
    narrow = model_width // groups
    col_start = ch_index * narrow

    def group_at(step):
        return lax.rem(ch_index + step + groups, groups) * narrow

    hidden_own = lax.dynamic_slice_in_dim(hidden, col_start, narrow, 1)
    hidden_own = spread(spread(hidden_own, "hi"), "lo").reshape(tokens, narrow)
    hidden_by_step = [hidden_own] + [turned(hidden_own, step) for step in range(1, groups)]
    clusters = cluster_weight.shape[1]
    share = cluster_weight.shape[0]
    ids = jnp.stack([cluster_id, target // 256, target % 256]).astype(BF)
    small = spread(jnp.concatenate([cluster_weight.reshape(-1), ids.reshape(-1)]), TOK)
    cluster_part = small[:, : share * clusters].reshape(model_width, clusters)
    ids = small[:, share * clusters :].astype(jnp.int32).reshape(owners // lo, lo, 3, local)
    ids = ids.transpose(2, 1, 0, 3).reshape(3, tokens)
    cluster_all, target_all = ids[0], ids[1] * 256 + ids[2]

    words = head_weight.shape[1] // owners
    word_part = lax.all_to_all(head_weight, TOK, split_axis=1, concat_axis=0, tiled=True)
    conv_part = lax.all_gather(conv_weight, "hi", axis=2, tiled=True)

    mine = (cluster_all >= 0) & (cluster_all // 2 == me)
    rank = running_count(mine.reshape(owners, local).astype(F32)).reshape(tokens)
    slot_ids = jnp.where(mine, rank.astype(jnp.int32) - 1, -1)
    chosen = slot_ids[:, None] == jnp.arange(slots, dtype=jnp.int32)[None, :]
    chosen_bf = chosen.astype(BF)
    rows = jnp.zeros((slots, model_width), BF)
    for step, part in enumerate(hidden_by_step):
        picked_part = t_dot(chosen_bf, part).astype(BF)
        rows = lax.dynamic_update_slice_in_dim(rows, picked_part, group_at(-step), 1)
    word_ids = jnp.sum(jnp.where(chosen, target_all[:, None], 0), axis=0)
    tiers = jnp.sum(jnp.where(chosen, cluster_all[:, None] % 2 + 1, 0), axis=0)
    first_member, second_member = tiers == 1, tiers == 2
    first_proj, second_proj = tail1_proj[0], tail2_proj[0]
    first_out, second_out = tail1_out[0], tail2_out[0]
    first_features, first_logits, first_hot, first_pick, first_stats = tier_start(
        rows, word_ids, first_proj, first_out, ch_index
    )
    second_features, second_logits, second_hot, second_pick, second_stats = tier_start(
        rows, word_ids, second_proj, second_out, ch_index
    )
    stats = lax.all_gather(jnp.stack([first_stats, second_stats], axis=1), "ch")
    top, total = merge_stats(stats)
    tail_log = top + jnp.log(total)
    first_slope = tier_slope(first_logits, first_hot, first_member, tail_log[0])
    second_slope = tier_slope(second_logits, second_hot, second_member, tail_log[1])
    dz = jnp.concatenate(
        [dot_t(first_slope, first_out), dot_t(second_slope, second_out)], axis=1
    )
    dz = jnp.sum(lax.all_gather(dz, "ch"), axis=0).astype(BF)
    first_dz = dz[:, : first_proj.shape[1]]
    second_dz = dz[:, first_proj.shape[1] :]
    first_own = lax.dynamic_slice_in_dim(first_proj, col_start, narrow, 0)
    second_own = lax.dynamic_slice_in_dim(second_proj, col_start, narrow, 0)
    back = (dot_t(first_dz, first_own) + dot_t(second_dz, second_own)).astype(BF)
    once = jnp.where(ch_index == 0, 1.0, 0.0)
    tail_loss = jnp.where(first_member, once * tail_log[0] - first_pick, 0.0)
    tail_loss = tail_loss + jnp.where(second_member, once * tail_log[1] - second_pick, 0.0)
    first_out_grad = t_dot(first_features, first_slope)
    second_out_grad = t_dot(second_features, second_slope)
    rows_part = lax.dynamic_slice_in_dim(rows, col_start, narrow, 1)
    first_proj_grad = t_dot(rows_part, first_dz)
    second_proj_grad = t_dot(rows_part, second_dz)

    spare = -(words + clusters) % LANES
    columns = jnp.concatenate(
        [word_part, cluster_part, jnp.zeros((model_width, spare), BF)], axis=1
    )
    place = jnp.arange(columns.shape[1], dtype=jnp.int32)[None, :]
    limit = jnp.where(me == 0, words + clusters, words)
    logits = sum(
        dot(part, lax.dynamic_slice_in_dim(columns, group_at(-step), narrow, 0))
        for step, part in enumerate(hidden_by_step)
    )
    logits = jnp.where(place < limit, logits, -jnp.inf)
    top = jnp.max(logits, axis=1)
    total = jnp.sum(jnp.exp(logits - top[:, None]), axis=1)
    is_tail = cluster_all >= 0
    word_place = target_all - (ch_index * owners + me) * words
    word_place = jnp.where((word_place >= 0) & (word_place < words), word_place, -1)
    cluster_place = cluster_all - ch_index * clusters
    cluster_here = (cluster_place >= 0) & (cluster_place < clusters) & (me == 0)
    cluster_place = jnp.where(cluster_here, cluster_place + words, -1)
    hot = place == jnp.where(is_tail, cluster_place, word_place)[:, None]
    picked = jnp.sum(jnp.where(hot, logits, 0.0), axis=1)
    stats = lax.all_gather(jnp.stack([top, total]), "ch")
    stats = spread(jnp.stack(merge_stats(stats)), TOK)
    top, total = merge_stats(stats)
    head_log = top + jnp.log(total)
    head_log, conv_part = lax.optimization_barrier((head_log, conv_part))
    slope = (jnp.exp(logits - head_log[:, None]) - hot.astype(F32)).astype(BF)
    grad_sum = 0.0
    for step in range(1, groups):
        block = lax.dynamic_slice_in_dim(columns, group_at(step), narrow, 0)
        grad_sum = grad_sum + turned(dot_t(slope, block).astype(BF), step).astype(F32)
    block = lax.dynamic_slice_in_dim(columns, col_start, narrow, 0)
    own_part = dot_t(
        jnp.concatenate([slope, chosen_bf], axis=1), jnp.concatenate([block, back.T], axis=1)
    )
    grad_sum = (grad_sum + own_part).astype(BF).reshape(lo, owners // lo, local, narrow)
    grad_sum = jnp.sum(exchange(grad_sum, "lo").astype(F32), axis=0).astype(BF)
    grad_sum = jnp.sum(exchange(grad_sum, "hi").astype(F32), axis=0)

    loss_part = jnp.sum(jnp.where(chosen, tail_loss[None, :], 0.0), axis=1) - picked
    loss_part = loss_part.reshape(lo, owners // lo, local).transpose(1, 0, 2)
    loss_part = jnp.sum(exchange(loss_part.reshape(owners, local), TOK), axis=0)
    own_loss = jnp.sum(lax.all_gather(loss_part, "ch"), axis=0)
    own_log = lax.dynamic_index_in_dim(
        head_log.reshape(lo, owners // lo, local).transpose(1, 0, 2).reshape(owners, local),
        me,
        keepdims=False,
    )
    token_loss = own_loss + own_log

    gate_a = pre_gates[0].astype(F32)
    gate_sig = jax.nn.sigmoid(pre_gates[1].astype(F32))
    gate_grads = jnp.stack(
        [grad_sum * gate_sig, grad_sum * gate_a * gate_sig * (1.0 - gate_sig)]
    ).astype(BF)
    gates = spread(gate_grads, "lo")
    near = lo * local
    taps = conv_part.shape[1]
    reach = conv_part.shape[2]
    conv_terms = sum(
        dot_t(gates[:, half].reshape(near, narrow), conv_part[half].reshape(taps * reach, narrow))
        for half in range(2)
    ).reshape(near // LEN, LEN, taps * reach)
    conv_terms = sum(
        jnp.pad(
            conv_terms[:, tap:, tap * reach : (tap + 1) * reach], ((0, 0), (0, tap), (0, 0))
        )
        for tap in range(taps)
    ).astype(BF)
    conv_terms = exchange(conv_terms.reshape(lo, local, reach), "lo")
    conv_terms = conv_terms.reshape(lo, local, owners // lo, share).transpose(1, 2, 0, 3)
    conv_terms = conv_terms.reshape(local, model_width)
    conv_grad = lax.dynamic_slice_in_dim(conv_terms, col_start, narrow, 1).astype(F32)
    for step in range(1, groups):
        block = lax.dynamic_slice_in_dim(conv_terms, group_at(step), narrow, 1)
        conv_grad = conv_grad + turned(block, step).astype(F32)
    grad_input = (grad_sum + conv_grad).astype(BF)
    return (
        token_loss,
        grad_input,
        first_proj_grad[None],
        second_proj_grad[None],
        first_out_grad[None],
        second_out_grad[None],
    )


def solution(mesh):
    n_tok, n_ch = mesh.shape["tok"], mesh.shape["ch"]
    lo = 1
    while n_tok % (lo * 2) == 0 and lo * lo * 4 <= n_tok:
        lo *= 2
    split = Mesh(mesh.devices.reshape(n_tok // lo, lo, n_ch), ("hi", "lo", "ch"))
    placed = (
        P(TOK, None),
        P(None, TOK, "ch"),
        P(None, None, TOK, "ch"),
        P(TOK, "ch"),
        P(TOK, "ch"),
        P(TOK, None, None),
        P(TOK, None, None),
        P(TOK, None, "ch"),
        P(TOK, None, "ch"),
        P(TOK),
        P(TOK),
    )
    return jax.shard_map(
        on_device,
        mesh=split,
        in_specs=placed,
        out_specs=(
            P(TOK),
            P(TOK, "ch"),
            P(TOK, "ch", None),
            P(TOK, "ch", None),
            P(TOK, None, "ch"),
            P(TOK, None, "ch"),
        ),
        check_vma=False,
    )
```

```python
import jax
import jax.numpy as jnp
from jax import lax
from jax.experimental import pallas as pl
from jax.experimental.pallas import tpu as pltpu
from jax.sharding import Mesh, PartitionSpec as P

LEN = 128
LANES = 128
TOK = ("hi", "lo")
BF = jnp.bfloat16
F32 = jnp.float32


def dot(a, b):
    return jnp.dot(a, b, preferred_element_type=F32)


def dot_t(a, b):
    return lax.dot_general(a, b, (((1,), (1,)), ((), ())), preferred_element_type=F32)


def t_dot(a, b):
    return lax.dot_general(a, b, (((0,), (0,)), ((), ())), preferred_element_type=F32)


def merge_stats(stats):
    top = jnp.max(stats[:, 0], axis=0)
    total = jnp.sum(stats[:, 1] * jnp.exp(stats[:, 0] - top), axis=0)
    return top, total


def exchange(x, axis):
    return lax.all_to_all(x, axis, split_axis=0, concat_axis=0, tiled=True)


def spread(x, axis):
    return exchange(jnp.broadcast_to(x[None], (lax.axis_size(axis), *x.shape)), axis)


def turned(x, step):
    groups = lax.axis_size("ch")
    return lax.ppermute(x, "ch", [(k, (k + step) % groups) for k in range(groups)])


def around(name, step):
    size = lax.axis_size(name)
    return lax.rem(lax.axis_index(name) + (step + size), size)


def device(**moved):
    return {name: moved.get(name, lax.axis_index(name)) for name in ("hi", "lo", "ch")}


def tok_device(step):
    owners, lo = lax.axis_size(TOK), lax.axis_size("lo")
    me = lax.axis_index("hi") * lo + lax.axis_index("lo")
    peer = lax.rem(me + step, owners)
    return peer, device(hi=peer // lo, lo=lax.rem(peer, lo))


def greet(peers):
    barrier = pltpu.get_barrier_semaphore()
    for peer in peers:
        pl.semaphore_signal(barrier, inc=1, device_id=peer, device_id_type=pl.DeviceIdType.MESH)
    pl.semaphore_wait(barrier, len(peers))


def push(src, dst, send, recv, peer):
    copy = pltpu.make_async_remote_copy(
        src_ref=src,
        dst_ref=dst,
        send_sem=send,
        recv_sem=recv,
        device_id=peer,
        device_id_type=pl.DeviceIdType.MESH,
    )
    copy.start()
    return copy


def gather_kernel(
    hidden, small, words, hidden_out, small_out, words_out, hid_s, hid_r, ch_s, ch_r, sm_s, sm_r, w_s, w_r, own
):
    owners, his, los = lax.axis_size(TOK), lax.axis_size("hi"), lax.axis_size("lo")
    groups = lax.axis_size("ch")
    hi, lo, ch = lax.axis_index("hi"), lax.axis_index("lo"), lax.axis_index("ch")
    me = hi * los + lo
    share = words_out.shape[0] // owners
    width = words_out.shape[1]

    def chunk(peer):
        if len(words.shape) == 3:
            return words.at[peer]
        return words.at[:, pl.ds(pl.multiple_of(peer * width, LANES), width)]

    place = words_out.at[pl.ds(pl.multiple_of(me * share, share), share), :]
    locals_ = [
        pltpu.make_async_copy(hidden, hidden_out.at[ch, lo, hi], own.at[0]),
        pltpu.make_async_copy(small, small_out.at[me], own.at[1]),
        pltpu.make_async_copy(chunk(me), place, own.at[2]),
    ]
    for copy in locals_:
        copy.start()
    greet(
        [tok_device(step)[1] for step in range(1, owners)]
        + [device(ch=around("ch", step)) for step in range(1, groups)]
    )
    ends = []
    across = {}
    for a in range(1, his):
        peer = device(hi=around("hi", a))
        across[0, a] = push(
            hidden, hidden_out.at[ch, lo, hi], hid_s.at[0, a], hid_r.at[0, a], peer
        )
    for b in range(1, los):
        peer = device(lo=around("lo", b))
        across[b, 0] = push(
            hidden, hidden_out.at[ch, lo, hi], hid_s.at[b, 0], hid_r.at[b, 0], peer
        )
    for step in range(1, owners):
        peer = tok_device(step)[1]
        ends.append(push(small, small_out.at[me], sm_s.at[step], sm_r.at[step], peer))
    for step in range(1, owners):
        index, peer = tok_device(step)
        ends.append(push(chunk(index), place, w_s.at[step], w_r.at[step], peer))
    for a in range(1, his):
        across[0, a].wait_recv()
        block = hidden_out.at[ch, lo, around("hi", -a)]
        for b in range(1, los):
            peer = device(lo=around("lo", b))
            across[b, a] = push(block, block, hid_s.at[b, a], hid_r.at[b, a], peer)
    locals_[0].wait()
    for b in range(los):
        if b > 0:
            for a in range(his):
                across[b, a].wait_recv()
        block = hidden_out.at[ch, around("lo", -b)]
        for c in range(1, groups):
            peer = device(ch=around("ch", c))
            ends.append(push(block, block, ch_s.at[c, b], ch_r.at[c, b], peer))
    for copy in across.values():
        copy.wait_send()
    for copy in ends + locals_[1:]:
        copy.wait()


def gather(hidden, small, words):
    owners, his, los = lax.axis_size(TOK), lax.axis_size("hi"), lax.axis_size("lo")
    groups = lax.axis_size("ch")
    share = words.shape[0]
    width = words.shape[1] // owners
    if width % LANES:
        words = words.reshape(share, owners, width).transpose(1, 0, 2)
    dma = pltpu.SemaphoreType.DMA
    anywhere = pl.BlockSpec(memory_space=pl.ANY)
    return pl.pallas_call(
        gather_kernel,
        out_shape=(
            jax.ShapeDtypeStruct((groups, los, his, *hidden.shape), BF),
            jax.ShapeDtypeStruct((owners, *small.shape), BF),
            jax.ShapeDtypeStruct((owners * share, width), BF),
        ),
        in_specs=[anywhere] * 3,
        out_specs=(anywhere,) * 3,
        scratch_shapes=[
            dma((los, his)),
            dma((los, his)),
            dma((groups, los)),
            dma((groups, los)),
            dma((owners,)),
            dma((owners,)),
            dma((owners,)),
            dma((owners,)),
            dma((3,)),
        ],
        compiler_params=pltpu.CompilerParams(collective_id=0, has_side_effects=True),
    )(hidden, small, words)


def scatter_kernel(
    grad, gates, sum_out, gates_out, near, mid, far, own_gates, near_s, near_r, far_s, far_r, gate_s, gate_r, own
):
    his, los = lax.axis_size("hi"), lax.axis_size("lo")
    lo = lax.axis_index("lo")
    hi_peers = [device(hi=around("hi", a)) for a in range(1, his)]
    lo_peers = [device(lo=around("lo", b)) for b in range(1, los)]
    greet(hi_peers + lo_peers)
    order = list(range(1, his)) + [0]
    copies = {}
    for a in order:
        for b in range(1, los):
            copies[b, a] = push(
                grad.at[around("lo", b), around("hi", a)],
                near.at[b, a],
                near_s.at[b, a],
                near_r.at[b, a],
                lo_peers[b - 1],
            )
    outward = {}
    for a in order:
        total = grad[lo, around("hi", a)].astype(F32)
        for b in range(1, los):
            copies[b, a].wait_recv()
            total = total + near[b, a].astype(F32)
        if a > 0:
            mid[a] = total.astype(BF)
            outward[a] = push(mid.at[a], far.at[a], far_s.at[a], far_r.at[a], hi_peers[a - 1])
        else:
            sum_out[...] = total
    total = sum_out[...]
    for a in range(1, his):
        outward[a].wait_recv()
        total = total + far[a].astype(F32)
    sum_out[...] = total
    sig = jax.nn.sigmoid(gates[1].astype(F32))
    own_gates[0] = (total * sig).astype(BF)
    own_gates[1] = (total * gates[0].astype(F32) * sig * (1.0 - sig)).astype(BF)
    spreads = [
        push(own_gates, gates_out.at[lo], gate_s.at[b], gate_r.at[b], lo_peers[b - 1])
        for b in range(1, los)
    ]
    kept = pltpu.make_async_copy(own_gates, gates_out.at[lo], own)
    kept.start()
    for copy in list(copies.values()) + list(outward.values()):
        copy.wait_send()
    for copy in spreads:
        copy.wait()
    kept.wait()


def scatter(grad, gates):
    los, his, local, narrow = grad.shape
    dma = pltpu.SemaphoreType.DMA
    inside = pl.BlockSpec(memory_space=pltpu.VMEM)
    return pl.pallas_call(
        scatter_kernel,
        out_shape=(
            jax.ShapeDtypeStruct((local, narrow), F32),
            jax.ShapeDtypeStruct((los, *gates.shape), BF),
        ),
        in_specs=[inside] * 2,
        out_specs=(inside, pl.BlockSpec(memory_space=pl.ANY)),
        scratch_shapes=[
            pltpu.VMEM((los, his, local, narrow), BF),
            pltpu.VMEM((his, local, narrow), BF),
            pltpu.VMEM((his, local, narrow), BF),
            pltpu.VMEM(gates.shape, BF),
            dma((los, his)),
            dma((los, his)),
            dma((his,)),
            dma((his,)),
            dma((los,)),
            dma((los,)),
            dma,
        ],
        compiler_params=pltpu.CompilerParams(
            collective_id=1, has_side_effects=True, vmem_limit_bytes=24 << 20
        ),
    )(grad, gates)


def running_count(mine):
    local = mine.shape[1]
    upto = (jnp.arange(local)[:, None] <= jnp.arange(local)[None, :]).astype(F32)
    within = dot(mine, upto)
    blocks = mine.shape[0]
    before = (jnp.arange(blocks)[None, :] < jnp.arange(blocks)[:, None]).astype(F32)
    return within + dot(before, within[:, -1:])


def tier_start(rows, word_ids, proj, out_shard, ch_index):
    features = dot(rows, proj).astype(BF)
    logits = dot(features, out_shard)
    top = jnp.max(logits, axis=1)
    total = jnp.sum(jnp.exp(logits - top[:, None]), axis=1)
    width = out_shard.shape[1]
    positions = jnp.arange(width, dtype=jnp.int32) + ch_index * width
    hot = positions[None, :] == word_ids[:, None]
    picked = jnp.sum(jnp.where(hot, logits, 0.0), axis=1)
    return features, logits, hot, picked, jnp.stack([top, total])


def tier_slope(logits, hot, member, log_total):
    slope = jnp.exp(logits - log_total[:, None]) - hot.astype(F32)
    return jnp.where(member[:, None], slope, 0.0).astype(BF)


def on_device(
    hidden,
    pre_gates,
    conv_weight,
    head_weight,
    cluster_weight,
    tail1_proj,
    tail2_proj,
    tail1_out,
    tail2_out,
    cluster_id,
    target,
):
    local, model_width = hidden.shape
    owners = lax.axis_size(TOK)
    groups = lax.axis_size("ch")
    lo = lax.axis_size("lo")
    me = lax.axis_index(TOK)
    ch_index = lax.axis_index("ch")
    tokens = local * owners
    slots = max(2, local // owners) * owners
    narrow = model_width // groups
    col_start = ch_index * narrow

    def group_at(step):
        return lax.rem(ch_index + step + groups, groups) * narrow

    hidden_own = lax.dynamic_slice_in_dim(hidden, col_start, narrow, 1)
    clusters = cluster_weight.shape[1]
    share = cluster_weight.shape[0]
    ids = jnp.stack([cluster_id, target // 256, target % 256]).astype(BF)
    small = jnp.concatenate([cluster_weight.reshape(-1), ids.reshape(-1)])
    used = small.shape[0]
    small = jnp.pad(small, (0, -used % (16 * LANES))).reshape(-1, LANES)
    hidden_all, small, word_part = gather(hidden_own, small, head_weight)
    hidden_by_step = [
        lax.dynamic_index_in_dim(hidden_all, around("ch", -step), keepdims=False).reshape(
            tokens, narrow
        )
        for step in range(groups)
    ]
    small = small.reshape(owners, -1)
    cluster_part = small[:, : share * clusters].reshape(model_width, clusters)
    ids = small[:, share * clusters : used].astype(jnp.int32).reshape(owners // lo, lo, 3, local)
    ids = ids.transpose(2, 1, 0, 3).reshape(3, tokens)
    cluster_all, target_all = ids[0], ids[1] * 256 + ids[2]

    words = head_weight.shape[1] // owners
    conv_weight, word_part = lax.optimization_barrier((conv_weight, word_part))
    conv_part = lax.all_gather(conv_weight, "hi", axis=2, tiled=True)

    mine = (cluster_all >= 0) & (cluster_all // 2 == me)
    rank = running_count(mine.reshape(owners, local).astype(F32)).reshape(tokens)
    slot_ids = jnp.where(mine, rank.astype(jnp.int32) - 1, -1)
    chosen = slot_ids[:, None] == jnp.arange(slots, dtype=jnp.int32)[None, :]
    chosen_bf = chosen.astype(BF)
    rows = jnp.zeros((slots, model_width), BF)
    for step, part in enumerate(hidden_by_step):
        picked_part = t_dot(chosen_bf, part).astype(BF)
        rows = lax.dynamic_update_slice_in_dim(rows, picked_part, group_at(-step), 1)
    word_ids = jnp.sum(jnp.where(chosen, target_all[:, None], 0), axis=0)
    tiers = jnp.sum(jnp.where(chosen, cluster_all[:, None] % 2 + 1, 0), axis=0)
    first_member, second_member = tiers == 1, tiers == 2
    first_proj, second_proj = tail1_proj[0], tail2_proj[0]
    first_out, second_out = tail1_out[0], tail2_out[0]
    first_features, first_logits, first_hot, first_pick, first_stats = tier_start(
        rows, word_ids, first_proj, first_out, ch_index
    )
    second_features, second_logits, second_hot, second_pick, second_stats = tier_start(
        rows, word_ids, second_proj, second_out, ch_index
    )
    stats = lax.all_gather(jnp.stack([first_stats, second_stats], axis=1), "ch")
    top, total = merge_stats(stats)
    tail_log = top + jnp.log(total)
    first_slope = tier_slope(first_logits, first_hot, first_member, tail_log[0])
    second_slope = tier_slope(second_logits, second_hot, second_member, tail_log[1])
    dz = jnp.concatenate(
        [dot_t(first_slope, first_out), dot_t(second_slope, second_out)], axis=1
    )
    dz = jnp.sum(lax.all_gather(dz, "ch"), axis=0).astype(BF)
    first_dz = dz[:, : first_proj.shape[1]]
    second_dz = dz[:, first_proj.shape[1] :]
    first_own = lax.dynamic_slice_in_dim(first_proj, col_start, narrow, 0)
    second_own = lax.dynamic_slice_in_dim(second_proj, col_start, narrow, 0)
    back = (dot_t(first_dz, first_own) + dot_t(second_dz, second_own)).astype(BF)
    once = jnp.where(ch_index == 0, 1.0, 0.0)
    tail_loss = jnp.where(first_member, once * tail_log[0] - first_pick, 0.0)
    tail_loss = tail_loss + jnp.where(second_member, once * tail_log[1] - second_pick, 0.0)
    first_out_grad = t_dot(first_features, first_slope)
    second_out_grad = t_dot(second_features, second_slope)
    rows_part = lax.dynamic_slice_in_dim(rows, col_start, narrow, 1)
    first_proj_grad = t_dot(rows_part, first_dz)
    second_proj_grad = t_dot(rows_part, second_dz)

    spare = -(words + clusters) % LANES
    columns = jnp.concatenate(
        [word_part, cluster_part, jnp.zeros((model_width, spare), BF)], axis=1
    )
    place = jnp.arange(columns.shape[1], dtype=jnp.int32)[None, :]
    limit = jnp.where(me == 0, words + clusters, words)
    logits = sum(
        dot(part, lax.dynamic_slice_in_dim(columns, group_at(-step), narrow, 0))
        for step, part in enumerate(hidden_by_step)
    )
    logits = jnp.where(place < limit, logits, -jnp.inf)
    top = jnp.max(logits, axis=1)
    total = jnp.sum(jnp.exp(logits - top[:, None]), axis=1)
    is_tail = cluster_all >= 0
    word_place = target_all - (ch_index * owners + me) * words
    word_place = jnp.where((word_place >= 0) & (word_place < words), word_place, -1)
    cluster_place = cluster_all - ch_index * clusters
    cluster_here = (cluster_place >= 0) & (cluster_place < clusters) & (me == 0)
    cluster_place = jnp.where(cluster_here, cluster_place + words, -1)
    hot = place == jnp.where(is_tail, cluster_place, word_place)[:, None]
    picked = jnp.sum(jnp.where(hot, logits, 0.0), axis=1)
    stats = lax.all_gather(jnp.stack([top, total]), "ch")
    stats = spread(jnp.stack(merge_stats(stats)), TOK)
    top, total = merge_stats(stats)
    head_log = top + jnp.log(total)
    head_log, conv_part = lax.optimization_barrier((head_log, conv_part))
    slope = (jnp.exp(logits - head_log[:, None]) - hot.astype(F32)).astype(BF)
    grad_sum = 0.0
    for step in range(1, groups):
        block = lax.dynamic_slice_in_dim(columns, group_at(step), narrow, 0)
        grad_sum = grad_sum + turned(dot_t(slope, block).astype(BF), step).astype(F32)
    block = lax.dynamic_slice_in_dim(columns, col_start, narrow, 0)
    own_part = dot_t(
        jnp.concatenate([slope, chosen_bf], axis=1), jnp.concatenate([block, back.T], axis=1)
    )
    grad_sum = (grad_sum + own_part).astype(BF).reshape(lo, owners // lo, local, narrow)
    grad_sum, gates = scatter(grad_sum, pre_gates)

    loss_part = jnp.sum(jnp.where(chosen, tail_loss[None, :], 0.0), axis=1) - picked
    loss_part = loss_part.reshape(lo, owners // lo, local).transpose(1, 0, 2)
    loss_part = jnp.sum(exchange(loss_part.reshape(owners, local), TOK), axis=0)
    own_loss = jnp.sum(lax.all_gather(loss_part, "ch"), axis=0)
    own_log = lax.dynamic_index_in_dim(
        head_log.reshape(lo, owners // lo, local).transpose(1, 0, 2).reshape(owners, local),
        me,
        keepdims=False,
    )
    token_loss = own_loss + own_log

    near = lo * local
    taps = conv_part.shape[1]
    reach = conv_part.shape[2]
    conv_terms = sum(
        dot_t(gates[:, half].reshape(near, narrow), conv_part[half].reshape(taps * reach, narrow))
        for half in range(2)
    ).reshape(near // LEN, LEN, taps * reach)
    conv_terms = sum(
        jnp.pad(
            conv_terms[:, tap:, tap * reach : (tap + 1) * reach], ((0, 0), (0, tap), (0, 0))
        )
        for tap in range(taps)
    ).astype(BF)
    conv_terms = exchange(conv_terms.reshape(lo, local, reach), "lo")
    conv_terms = conv_terms.reshape(lo, local, owners // lo, share).transpose(1, 2, 0, 3)
    conv_terms = conv_terms.reshape(local, model_width)
    conv_grad = lax.dynamic_slice_in_dim(conv_terms, col_start, narrow, 1).astype(F32)
    for step in range(1, groups):
        block = lax.dynamic_slice_in_dim(conv_terms, group_at(step), narrow, 1)
        conv_grad = conv_grad + turned(block, step).astype(F32)
    grad_input = (grad_sum + conv_grad).astype(BF)
    return (
        token_loss,
        grad_input,
        first_proj_grad[None],
        second_proj_grad[None],
        first_out_grad[None],
        second_out_grad[None],
    )


def solution(mesh):
    n_tok, n_ch = mesh.shape["tok"], mesh.shape["ch"]
    lo = 1
    while n_tok % (lo * 2) == 0 and lo * lo * 4 <= n_tok:
        lo *= 2
    split = Mesh(mesh.devices.reshape(n_tok // lo, lo, n_ch), ("hi", "lo", "ch"))
    placed = (
        P(TOK, None),
        P(None, TOK, "ch"),
        P(None, None, TOK, "ch"),
        P(TOK, "ch"),
        P(TOK, "ch"),
        P(TOK, None, None),
        P(TOK, None, None),
        P(TOK, None, "ch"),
        P(TOK, None, "ch"),
        P(TOK),
        P(TOK),
    )
    return jax.shard_map(
        on_device,
        mesh=split,
        in_specs=placed,
        out_specs=(
            P(TOK),
            P(TOK, "ch"),
            P(TOK, "ch", None),
            P(TOK, "ch", None),
            P(TOK, None, "ch"),
            P(TOK, None, "ch"),
        ),
        check_vma=False,
    )
```

```python
import jax
import jax.numpy as jnp
from jax import lax
from jax.experimental import pallas as pl
from jax.experimental.pallas import tpu as pltpu
from jax.sharding import Mesh, PartitionSpec as P

LEN = 128
LANES = 128
TOK = ("hi", "lo")
BF = jnp.bfloat16
F32 = jnp.float32


def dot(a, b):
    return jnp.dot(a, b, preferred_element_type=F32)


def dot_t(a, b):
    return lax.dot_general(a, b, (((1,), (1,)), ((), ())), preferred_element_type=F32)


def t_dot(a, b):
    return lax.dot_general(a, b, (((0,), (0,)), ((), ())), preferred_element_type=F32)


def merge_stats(stats):
    top = jnp.max(stats[:, 0], axis=0)
    total = jnp.sum(stats[:, 1] * jnp.exp(stats[:, 0] - top), axis=0)
    return top, total


def exchange(x, axis):
    return lax.all_to_all(x, axis, split_axis=0, concat_axis=0, tiled=True)


def spread(x, axis):
    return exchange(jnp.broadcast_to(x[None], (lax.axis_size(axis), *x.shape)), axis)


def turned(x, step):
    groups = lax.axis_size("ch")
    return lax.ppermute(x, "ch", [(k, (k + step) % groups) for k in range(groups)])


def around(name, step):
    size = lax.axis_size(name)
    return lax.rem(lax.axis_index(name) + (step + size), size)


def device(**moved):
    return {name: moved.get(name, lax.axis_index(name)) for name in ("hi", "lo", "ch")}


def tok_device(step):
    owners, lo = lax.axis_size(TOK), lax.axis_size("lo")
    me = lax.axis_index("hi") * lo + lax.axis_index("lo")
    peer = lax.rem(me + step, owners)
    return peer, device(hi=peer // lo, lo=lax.rem(peer, lo))


def greet(peers):
    barrier = pltpu.get_barrier_semaphore()
    for peer in peers:
        pl.semaphore_signal(barrier, inc=1, device_id=peer, device_id_type=pl.DeviceIdType.MESH)
    pl.semaphore_wait(barrier, len(peers))


def push(src, dst, send, recv, peer):
    copy = pltpu.make_async_remote_copy(
        src_ref=src,
        dst_ref=dst,
        send_sem=send,
        recv_sem=recv,
        device_id=peer,
        device_id_type=pl.DeviceIdType.MESH,
    )
    copy.start()
    return copy


def gather_kernel(
    hidden, small, words, hidden_out, small_out, words_out, hid_s, hid_r, ch_s, ch_r, sm_s, sm_r, w_s, w_r, own
):
    owners, his, los = lax.axis_size(TOK), lax.axis_size("hi"), lax.axis_size("lo")
    groups = lax.axis_size("ch")
    hi, lo, ch = lax.axis_index("hi"), lax.axis_index("lo"), lax.axis_index("ch")
    me = hi * los + lo
    share = words_out.shape[0] // owners
    width = words_out.shape[1]

    def chunk(peer):
        if len(words.shape) == 3:
            return words.at[peer]
        return words.at[:, pl.ds(pl.multiple_of(peer * width, LANES), width)]

    place = words_out.at[pl.ds(pl.multiple_of(me * share, share), share), :]
    locals_ = [
        pltpu.make_async_copy(hidden, hidden_out.at[ch, lo, hi], own.at[0]),
        pltpu.make_async_copy(small, small_out.at[me], own.at[1]),
        pltpu.make_async_copy(chunk(me), place, own.at[2]),
    ]
    for copy in locals_:
        copy.start()
    greet(
        [tok_device(step)[1] for step in range(1, owners)]
        + [device(ch=around("ch", step)) for step in range(1, groups)]
    )
    ends = []
    across = {}
    for a in range(1, his):
        peer = device(hi=around("hi", a))
        across[0, a] = push(
            hidden, hidden_out.at[ch, lo, hi], hid_s.at[0, a], hid_r.at[0, a], peer
        )
    for b in range(1, los):
        peer = device(lo=around("lo", b))
        across[b, 0] = push(
            hidden, hidden_out.at[ch, lo, hi], hid_s.at[b, 0], hid_r.at[b, 0], peer
        )
    for step in range(1, owners):
        peer = tok_device(step)[1]
        ends.append(push(small, small_out.at[me], sm_s.at[step], sm_r.at[step], peer))
    for step in range(1, owners):
        index, peer = tok_device(step)
        ends.append(push(chunk(index), place, w_s.at[step], w_r.at[step], peer))
    for a in range(1, his):
        across[0, a].wait_recv()
        block = hidden_out.at[ch, lo, around("hi", -a)]
        for b in range(1, los):
            peer = device(lo=around("lo", b))
            across[b, a] = push(block, block, hid_s.at[b, a], hid_r.at[b, a], peer)
    locals_[0].wait()
    for b in range(los):
        if b > 0:
            for a in range(his):
                across[b, a].wait_recv()
        block = hidden_out.at[ch, around("lo", -b)]
        for c in range(1, groups):
            peer = device(ch=around("ch", c))
            ends.append(push(block, block, ch_s.at[c, b], ch_r.at[c, b], peer))
    for copy in across.values():
        copy.wait_send()
    for copy in ends + locals_[1:]:
        copy.wait()


def gather(hidden, small, words):
    owners, his, los = lax.axis_size(TOK), lax.axis_size("hi"), lax.axis_size("lo")
    groups = lax.axis_size("ch")
    share = words.shape[0]
    width = words.shape[1] // owners
    if width % LANES:
        words = words.reshape(share, owners, width).transpose(1, 0, 2)
    dma = pltpu.SemaphoreType.DMA
    anywhere = pl.BlockSpec(memory_space=pl.ANY)
    return pl.pallas_call(
        gather_kernel,
        out_shape=(
            jax.ShapeDtypeStruct((groups, los, his, *hidden.shape), BF),
            jax.ShapeDtypeStruct((owners, *small.shape), BF),
            jax.ShapeDtypeStruct((owners * share, width), BF),
        ),
        in_specs=[anywhere] * 3,
        out_specs=(anywhere,) * 3,
        scratch_shapes=[
            dma((los, his)),
            dma((los, his)),
            dma((groups, los)),
            dma((groups, los)),
            dma((owners,)),
            dma((owners,)),
            dma((owners,)),
            dma((owners,)),
            dma((3,)),
        ],
        compiler_params=pltpu.CompilerParams(collective_id=0, has_side_effects=True),
    )(hidden, small, words)


def scatter_kernel(
    grad,
    gates,
    conv,
    loss,
    sum_out,
    conv_out,
    loss_out,
    near,
    mid,
    far,
    own_gates,
    all_gates,
    terms_out,
    loss_near,
    loss_mid,
    loss_far,
    near_s,
    near_r,
    far_s,
    far_r,
    gate_s,
    gate_r,
    term_s,
    term_r,
    ln_s,
    ln_r,
    lf_s,
    lf_r,
    own,
):
    his, los = lax.axis_size("hi"), lax.axis_size("lo")
    hi, lo = lax.axis_index("hi"), lax.axis_index("lo")
    hi_peers = [device(hi=around("hi", a)) for a in range(1, his)]
    lo_peers = [device(lo=around("lo", b)) for b in range(1, los)]
    local = sum_out.shape[0]
    reach = conv_out.shape[2]
    greet(hi_peers + lo_peers)
    order = list(range(1, his)) + [0]
    copies = {}
    ends = []
    for b in range(1, los):
        copies["loss", b] = push(
            loss.at[around("lo", b)], loss_near.at[b], ln_s.at[b], ln_r.at[b], lo_peers[b - 1]
        )
    for a in order:
        for b in range(1, los):
            copies[b, a] = push(
                grad.at[around("lo", b), around("hi", a)],
                near.at[b, a],
                near_s.at[b, a],
                near_r.at[b, a],
                lo_peers[b - 1],
            )
    outward = {}
    loss_sum = loss[lo]
    for b in range(1, los):
        copies["loss", b].wait_recv()
        loss_sum = loss_sum + loss_near[b]
    loss_mid[...] = loss_sum
    for a in range(1, his):
        outward["loss", a] = push(
            loss_mid.at[around("hi", a)], loss_far.at[a], lf_s.at[a], lf_r.at[a], hi_peers[a - 1]
        )
    for a in order:
        total = grad[lo, around("hi", a)].astype(F32)
        for b in range(1, los):
            copies[b, a].wait_recv()
            total = total + near[b, a].astype(F32)
        if a > 0:
            mid[a] = total.astype(BF)
            outward[a] = push(mid.at[a], far.at[a], far_s.at[a], far_r.at[a], hi_peers[a - 1])
        else:
            sum_out[...] = total
    own_loss = loss_mid[hi]
    total = sum_out[...]
    for a in range(1, his):
        outward["loss", a].wait_recv()
        own_loss = own_loss + loss_far[a]
        outward[a].wait_recv()
        total = total + far[a].astype(F32)
    loss_out[...] = own_loss
    sum_out[...] = total
    sig = jax.nn.sigmoid(gates[1].astype(F32))
    own_gates[0] = (total * sig).astype(BF)
    own_gates[1] = (total * gates[0].astype(F32) * sig * (1.0 - sig)).astype(BF)
    spreads = [
        push(own_gates, all_gates.at[b], gate_s.at[b], gate_r.at[b], lo_peers[b - 1])
        for b in range(1, los)
    ]
    rows = lax.broadcasted_iota(jnp.int32, (local, reach), 0) % LEN
    for b in range(los):
        if b > 0:
            spreads[b - 1].wait_recv()
            part = all_gates.at[b]
        else:
            part = own_gates
        wide = dot_t(part[0], conv[0]) + dot_t(part[1], conv[1])
        terms = wide[:, :reach]
        for tap in range(1, wide.shape[1] // reach):
            moved = pltpu.roll(wide[:, tap * reach : (tap + 1) * reach], local - tap, 0)
            terms = terms + jnp.where(rows < LEN - tap, moved, 0.0)
        terms_out[b] = terms.astype(BF)
        if b > 0:
            peer = device(lo=around("lo", -b))
            ends.append(
                push(terms_out.at[b], conv_out.at[lo], term_s.at[b], term_r.at[b], peer)
            )
        else:
            kept = pltpu.make_async_copy(terms_out.at[0], conv_out.at[lo], own)
            kept.start()
    for copy in list(copies.values()) + list(outward.values()) + spreads:
        copy.wait_send()
    for copy in ends:
        copy.wait()
    kept.wait()


def scatter(grad, gates, conv, loss):
    los, his, local, narrow = grad.shape
    halves, taps, reach, _ = conv.shape
    conv = conv.reshape(halves, taps * reach, narrow)
    loss = jnp.broadcast_to(loss.reshape(los, his, 1, local), (los, his, 8, local))
    dma = pltpu.SemaphoreType.DMA
    inside = pl.BlockSpec(memory_space=pltpu.VMEM)
    return pl.pallas_call(
        scatter_kernel,
        out_shape=(
            jax.ShapeDtypeStruct((local, narrow), F32),
            jax.ShapeDtypeStruct((los, local, reach), BF),
            jax.ShapeDtypeStruct((8, local), F32),
        ),
        in_specs=[inside] * 4,
        out_specs=(inside, pl.BlockSpec(memory_space=pl.ANY), inside),
        scratch_shapes=[
            pltpu.VMEM((los, his, local, narrow), BF),
            pltpu.VMEM((his, local, narrow), BF),
            pltpu.VMEM((his, local, narrow), BF),
            pltpu.VMEM(gates.shape, BF),
            pltpu.VMEM((los, *gates.shape), BF),
            pltpu.VMEM((los, local, reach), BF),
            pltpu.VMEM((los, his, 8, local), F32),
            pltpu.VMEM((his, 8, local), F32),
            pltpu.VMEM((his, 8, local), F32),
            dma((los, his)),
            dma((los, his)),
            dma((his,)),
            dma((his,)),
            dma((los,)),
            dma((los,)),
            dma((los,)),
            dma((los,)),
            dma((los,)),
            dma((los,)),
            dma((his,)),
            dma((his,)),
            dma,
        ],
        compiler_params=pltpu.CompilerParams(
            collective_id=1, has_side_effects=True, vmem_limit_bytes=32 << 20
        ),
    )(grad, gates, conv, loss)


def running_count(mine):
    local = mine.shape[1]
    upto = (jnp.arange(local)[:, None] <= jnp.arange(local)[None, :]).astype(F32)
    within = dot(mine, upto)
    blocks = mine.shape[0]
    before = (jnp.arange(blocks)[None, :] < jnp.arange(blocks)[:, None]).astype(F32)
    return within + dot(before, within[:, -1:])


def tier_start(rows, word_ids, proj, out_shard, ch_index):
    features = dot(rows, proj).astype(BF)
    logits = dot(features, out_shard)
    top = jnp.max(logits, axis=1)
    total = jnp.sum(jnp.exp(logits - top[:, None]), axis=1)
    width = out_shard.shape[1]
    positions = jnp.arange(width, dtype=jnp.int32) + ch_index * width
    hot = positions[None, :] == word_ids[:, None]
    picked = jnp.sum(jnp.where(hot, logits, 0.0), axis=1)
    return features, logits, hot, picked, jnp.stack([top, total])


def tier_slope(logits, hot, member, log_total):
    slope = jnp.exp(logits - log_total[:, None]) - hot.astype(F32)
    return jnp.where(member[:, None], slope, 0.0).astype(BF)


def on_device(
    hidden,
    pre_gates,
    conv_weight,
    head_weight,
    cluster_weight,
    tail1_proj,
    tail2_proj,
    tail1_out,
    tail2_out,
    cluster_id,
    target,
):
    local, model_width = hidden.shape
    owners = lax.axis_size(TOK)
    groups = lax.axis_size("ch")
    lo = lax.axis_size("lo")
    me = lax.axis_index(TOK)
    ch_index = lax.axis_index("ch")
    tokens = local * owners
    slots = max(2, local // owners) * owners
    narrow = model_width // groups
    col_start = ch_index * narrow

    def group_at(step):
        return lax.rem(ch_index + step + groups, groups) * narrow

    hidden_own = lax.dynamic_slice_in_dim(hidden, col_start, narrow, 1)
    clusters = cluster_weight.shape[1]
    share = cluster_weight.shape[0]
    ids = jnp.stack([cluster_id, target // 256, target % 256]).astype(BF)
    small = jnp.concatenate([cluster_weight.reshape(-1), ids.reshape(-1)])
    used = small.shape[0]
    small = jnp.pad(small, (0, -used % (16 * LANES))).reshape(-1, LANES)
    hidden_all, small, word_part = gather(hidden_own, small, head_weight)
    hidden_by_step = [
        lax.dynamic_index_in_dim(hidden_all, around("ch", -step), keepdims=False).reshape(
            tokens, narrow
        )
        for step in range(groups)
    ]
    small = small.reshape(owners, -1)
    cluster_part = small[:, : share * clusters].reshape(model_width, clusters)
    ids = small[:, share * clusters : used].astype(jnp.int32).reshape(owners // lo, lo, 3, local)
    ids = ids.transpose(2, 1, 0, 3).reshape(3, tokens)
    cluster_all, target_all = ids[0], ids[1] * 256 + ids[2]

    words = head_weight.shape[1] // owners
    conv_weight, word_part = lax.optimization_barrier((conv_weight, word_part))
    conv_part = lax.all_gather(conv_weight, "hi", axis=2, tiled=True)

    mine = (cluster_all >= 0) & (cluster_all // 2 == me)
    rank = running_count(mine.reshape(owners, local).astype(F32)).reshape(tokens)
    slot_ids = jnp.where(mine, rank.astype(jnp.int32) - 1, -1)
    chosen = slot_ids[:, None] == jnp.arange(slots, dtype=jnp.int32)[None, :]
    chosen_bf = chosen.astype(BF)
    rows = jnp.zeros((slots, model_width), BF)
    for step, part in enumerate(hidden_by_step):
        picked_part = t_dot(chosen_bf, part).astype(BF)
        rows = lax.dynamic_update_slice_in_dim(rows, picked_part, group_at(-step), 1)
    word_ids = jnp.sum(jnp.where(chosen, target_all[:, None], 0), axis=0)
    tiers = jnp.sum(jnp.where(chosen, cluster_all[:, None] % 2 + 1, 0), axis=0)
    first_member, second_member = tiers == 1, tiers == 2
    first_proj, second_proj = tail1_proj[0], tail2_proj[0]
    first_out, second_out = tail1_out[0], tail2_out[0]
    first_features, first_logits, first_hot, first_pick, first_stats = tier_start(
        rows, word_ids, first_proj, first_out, ch_index
    )
    second_features, second_logits, second_hot, second_pick, second_stats = tier_start(
        rows, word_ids, second_proj, second_out, ch_index
    )
    stats = lax.all_gather(jnp.stack([first_stats, second_stats], axis=1), "ch")
    top, total = merge_stats(stats)
    tail_log = top + jnp.log(total)
    first_slope = tier_slope(first_logits, first_hot, first_member, tail_log[0])
    second_slope = tier_slope(second_logits, second_hot, second_member, tail_log[1])
    dz = jnp.concatenate(
        [dot_t(first_slope, first_out), dot_t(second_slope, second_out)], axis=1
    )
    dz = jnp.sum(lax.all_gather(dz, "ch"), axis=0).astype(BF)
    first_dz = dz[:, : first_proj.shape[1]]
    second_dz = dz[:, first_proj.shape[1] :]
    first_own = lax.dynamic_slice_in_dim(first_proj, col_start, narrow, 0)
    second_own = lax.dynamic_slice_in_dim(second_proj, col_start, narrow, 0)
    back = (dot_t(first_dz, first_own) + dot_t(second_dz, second_own)).astype(BF)
    once = jnp.where(ch_index == 0, 1.0, 0.0)
    tail_loss = jnp.where(first_member, once * tail_log[0] - first_pick, 0.0)
    tail_loss = tail_loss + jnp.where(second_member, once * tail_log[1] - second_pick, 0.0)
    first_out_grad = t_dot(first_features, first_slope)
    second_out_grad = t_dot(second_features, second_slope)
    rows_part = lax.dynamic_slice_in_dim(rows, col_start, narrow, 1)
    first_proj_grad = t_dot(rows_part, first_dz)
    second_proj_grad = t_dot(rows_part, second_dz)

    spare = -(words + clusters) % LANES
    columns = jnp.concatenate(
        [word_part, cluster_part, jnp.zeros((model_width, spare), BF)], axis=1
    )
    place = jnp.arange(columns.shape[1], dtype=jnp.int32)[None, :]
    limit = jnp.where(me == 0, words + clusters, words)
    logits = sum(
        dot(part, lax.dynamic_slice_in_dim(columns, group_at(-step), narrow, 0))
        for step, part in enumerate(hidden_by_step)
    )
    logits = jnp.where(place < limit, logits, -jnp.inf)
    top = jnp.max(logits, axis=1)
    total = jnp.sum(jnp.exp(logits - top[:, None]), axis=1)
    is_tail = cluster_all >= 0
    word_place = target_all - (ch_index * owners + me) * words
    word_place = jnp.where((word_place >= 0) & (word_place < words), word_place, -1)
    cluster_place = cluster_all - ch_index * clusters
    cluster_here = (cluster_place >= 0) & (cluster_place < clusters) & (me == 0)
    cluster_place = jnp.where(cluster_here, cluster_place + words, -1)
    hot = place == jnp.where(is_tail, cluster_place, word_place)[:, None]
    picked = jnp.sum(jnp.where(hot, logits, 0.0), axis=1)
    stats = lax.all_gather(jnp.stack([top, total]), "ch")
    stats = spread(jnp.stack(merge_stats(stats)), TOK)
    top, total = merge_stats(stats)
    head_log = top + jnp.log(total)
    slope = (jnp.exp(logits - head_log[:, None]) - hot.astype(F32)).astype(BF)
    grad_sum = 0.0
    for step in range(1, groups):
        block = lax.dynamic_slice_in_dim(columns, group_at(step), narrow, 0)
        grad_sum = grad_sum + turned(dot_t(slope, block).astype(BF), step).astype(F32)
    block = lax.dynamic_slice_in_dim(columns, col_start, narrow, 0)
    own_part = dot_t(
        jnp.concatenate([slope, chosen_bf], axis=1), jnp.concatenate([block, back.T], axis=1)
    )
    grad_sum = (grad_sum + own_part).astype(BF).reshape(lo, owners // lo, local, narrow)
    loss_part = jnp.sum(jnp.where(chosen, tail_loss[None, :], 0.0), axis=1) - picked
    grad_sum, conv_terms, own_loss = scatter(grad_sum, pre_gates, conv_part, loss_part)
    own_loss = jnp.sum(lax.all_gather(own_loss[0], "ch"), axis=0)
    own_log = lax.dynamic_index_in_dim(
        head_log.reshape(lo, owners // lo, local).transpose(1, 0, 2).reshape(owners, local),
        me,
        keepdims=False,
    )
    token_loss = own_loss + own_log

    conv_terms = conv_terms.reshape(lo, local, owners // lo, share).transpose(1, 2, 0, 3)
    conv_terms = conv_terms.reshape(local, model_width)
    conv_grad = lax.dynamic_slice_in_dim(conv_terms, col_start, narrow, 1).astype(F32)
    for step in range(1, groups):
        block = lax.dynamic_slice_in_dim(conv_terms, group_at(step), narrow, 1)
        conv_grad = conv_grad + turned(block, step).astype(F32)
    grad_input = (grad_sum + conv_grad).astype(BF)
    return (
        token_loss,
        grad_input,
        first_proj_grad[None],
        second_proj_grad[None],
        first_out_grad[None],
        second_out_grad[None],
    )


def solution(mesh):
    n_tok, n_ch = mesh.shape["tok"], mesh.shape["ch"]
    lo = 1
    while n_tok % (lo * 2) == 0 and lo * lo * 4 <= n_tok:
        lo *= 2
    split = Mesh(mesh.devices.reshape(n_tok // lo, lo, n_ch), ("hi", "lo", "ch"))
    placed = (
        P(TOK, None),
        P(None, TOK, "ch"),
        P(None, None, TOK, "ch"),
        P(TOK, "ch"),
        P(TOK, "ch"),
        P(TOK, None, None),
        P(TOK, None, None),
        P(TOK, None, "ch"),
        P(TOK, None, "ch"),
        P(TOK),
        P(TOK),
    )
    return jax.shard_map(
        on_device,
        mesh=split,
        in_specs=placed,
        out_specs=(
            P(TOK),
            P(TOK, "ch"),
            P(TOK, "ch", None),
            P(TOK, "ch", None),
            P(TOK, None, "ch"),
            P(TOK, None, "ch"),
        ),
        check_vma=False,
    )
```

```python
import jax
import jax.numpy as jnp
from jax import lax
from jax.experimental import pallas as pl
from jax.experimental.pallas import tpu as pltpu
from jax.sharding import Mesh, PartitionSpec as P

LEN = 128
LANES = 128
TOK = ("hi", "lo")
BF = jnp.bfloat16
F32 = jnp.float32


def dot(a, b):
    return jnp.dot(a, b, preferred_element_type=F32)


def dot_t(a, b):
    return lax.dot_general(a, b, (((1,), (1,)), ((), ())), preferred_element_type=F32)


def t_dot(a, b):
    return lax.dot_general(a, b, (((0,), (0,)), ((), ())), preferred_element_type=F32)


def merge_stats(stats):
    top = jnp.max(stats[:, 0], axis=0)
    total = jnp.sum(stats[:, 1] * jnp.exp(stats[:, 0] - top), axis=0)
    return top, total


def exchange(x, axis):
    return lax.all_to_all(x, axis, split_axis=0, concat_axis=0, tiled=True)


def spread(x, axis):
    return exchange(jnp.broadcast_to(x[None], (lax.axis_size(axis), *x.shape)), axis)


def turned(x, step):
    groups = lax.axis_size("ch")
    return lax.ppermute(x, "ch", [(k, (k + step) % groups) for k in range(groups)])


def around(name, step):
    size = lax.axis_size(name)
    return lax.rem(lax.axis_index(name) + (step + size), size)


def device(**moved):
    return {name: moved.get(name, lax.axis_index(name)) for name in ("hi", "lo", "ch")}


def tok_device(step):
    owners, lo = lax.axis_size(TOK), lax.axis_size("lo")
    me = lax.axis_index("hi") * lo + lax.axis_index("lo")
    peer = lax.rem(me + step, owners)
    return peer, device(hi=peer // lo, lo=lax.rem(peer, lo))


def greet(peers):
    barrier = pltpu.get_barrier_semaphore()
    for peer in peers:
        pl.semaphore_signal(barrier, inc=1, device_id=peer, device_id_type=pl.DeviceIdType.MESH)
    pl.semaphore_wait(barrier, len(peers))


def push(src, dst, send, recv, peer):
    copy = pltpu.make_async_remote_copy(
        src_ref=src,
        dst_ref=dst,
        send_sem=send,
        recv_sem=recv,
        device_id=peer,
        device_id_type=pl.DeviceIdType.MESH,
    )
    copy.start()
    return copy


def gather_kernel(
    hidden, small, words, hidden_out, small_out, words_out, hid_s, hid_r, ch_s, ch_r, sm_s, sm_r, w_s, w_r, own
):
    owners, his, los = lax.axis_size(TOK), lax.axis_size("hi"), lax.axis_size("lo")
    groups = lax.axis_size("ch")
    hi, lo = lax.axis_index("hi"), lax.axis_index("lo")
    me = hi * los + lo
    share = words_out.shape[0] // owners
    width = words_out.shape[1]

    def chunk(peer):
        if len(words.shape) == 3:
            return words.at[peer]
        return words.at[:, pl.ds(pl.multiple_of(peer * width, LANES), width)]

    place = words_out.at[pl.ds(pl.multiple_of(me * share, share), share), :]
    locals_ = [
        pltpu.make_async_copy(hidden, hidden_out.at[0, lo, hi], own.at[0]),
        pltpu.make_async_copy(small, small_out.at[me], own.at[1]),
        pltpu.make_async_copy(chunk(me), place, own.at[2]),
    ]
    for copy in locals_:
        copy.start()
    greet(
        [tok_device(step)[1] for step in range(1, owners)]
        + [device(ch=around("ch", step)) for step in range(1, groups)]
    )
    ends = []
    across = {}
    for a in range(1, his):
        peer = device(hi=around("hi", a))
        across[0, a] = push(
            hidden, hidden_out.at[0, lo, hi], hid_s.at[0, a], hid_r.at[0, a], peer
        )
    for b in range(1, los):
        peer = device(lo=around("lo", b))
        across[b, 0] = push(
            hidden, hidden_out.at[0, lo, hi], hid_s.at[b, 0], hid_r.at[b, 0], peer
        )
    for step in range(1, owners):
        peer = tok_device(step)[1]
        ends.append(push(small, small_out.at[me], sm_s.at[step], sm_r.at[step], peer))
    for step in range(1, owners):
        index, peer = tok_device(step)
        ends.append(push(chunk(index), place, w_s.at[step], w_r.at[step], peer))
    for a in range(1, his):
        across[0, a].wait_recv()
        block = hidden_out.at[0, lo, around("hi", -a)]
        for b in range(1, los):
            peer = device(lo=around("lo", b))
            across[b, a] = push(block, block, hid_s.at[b, a], hid_r.at[b, a], peer)
    locals_[0].wait()
    for b in range(los):
        if b > 0:
            for a in range(his):
                across[b, a].wait_recv()
        block = hidden_out.at[0, around("lo", -b)]
        for c in range(1, groups):
            peer = device(ch=around("ch", c))
            there = hidden_out.at[c, around("lo", -b)]
            ends.append(push(block, there, ch_s.at[c, b], ch_r.at[c, b], peer))
    for copy in across.values():
        copy.wait_send()
    for copy in ends + locals_[1:]:
        copy.wait()


def gather(hidden, small, words):
    owners, his, los = lax.axis_size(TOK), lax.axis_size("hi"), lax.axis_size("lo")
    groups = lax.axis_size("ch")
    share = words.shape[0]
    width = words.shape[1] // owners
    if width % LANES:
        words = words.reshape(share, owners, width).transpose(1, 0, 2)
    dma = pltpu.SemaphoreType.DMA
    anywhere = pl.BlockSpec(memory_space=pl.ANY)
    return pl.pallas_call(
        gather_kernel,
        out_shape=(
            jax.ShapeDtypeStruct((groups, los, his, *hidden.shape), BF),
            jax.ShapeDtypeStruct((owners, *small.shape), BF),
            jax.ShapeDtypeStruct((owners * share, width), BF),
        ),
        in_specs=[anywhere] * 3,
        out_specs=(anywhere,) * 3,
        scratch_shapes=[
            dma((los, his)),
            dma((los, his)),
            dma((groups, los)),
            dma((groups, los)),
            dma((owners,)),
            dma((owners,)),
            dma((owners,)),
            dma((owners,)),
            dma((3,)),
        ],
        compiler_params=pltpu.CompilerParams(collective_id=0, has_side_effects=True),
    )(hidden, small, words)


def scatter_kernel(
    grad,
    gates,
    conv_all,
    loss,
    sum_out,
    conv_out,
    loss_out,
    near,
    mid,
    far,
    own_gates,
    all_gates,
    terms_out,
    loss_near,
    loss_mid,
    loss_far,
    near_s,
    near_r,
    far_s,
    far_r,
    gate_s,
    gate_r,
    term_s,
    term_r,
    ln_s,
    ln_r,
    lf_s,
    lf_r,
    own,
    conv,
    conv_sem,
):
    conv_copy = pltpu.make_async_copy(conv_all, conv, conv_sem)
    conv_copy.start()
    his, los = lax.axis_size("hi"), lax.axis_size("lo")
    hi, lo = lax.axis_index("hi"), lax.axis_index("lo")
    hi_peers = [device(hi=around("hi", a)) for a in range(1, his)]
    lo_peers = [device(lo=around("lo", b)) for b in range(1, los)]
    local = sum_out.shape[0]
    reach = conv_out.shape[2]
    greet(hi_peers + lo_peers)
    order = list(range(1, his)) + [0]
    copies = {}
    ends = []
    for b in range(1, los):
        copies["loss", b] = push(
            loss.at[around("lo", b)], loss_near.at[b], ln_s.at[b], ln_r.at[b], lo_peers[b - 1]
        )
    for a in order:
        for b in range(1, los):
            copies[b, a] = push(
                grad.at[around("lo", b), around("hi", a)],
                near.at[b, a],
                near_s.at[b, a],
                near_r.at[b, a],
                lo_peers[b - 1],
            )
    outward = {}
    loss_sum = loss[lo]
    for b in range(1, los):
        copies["loss", b].wait_recv()
        loss_sum = loss_sum + loss_near[b]
    loss_mid[...] = loss_sum
    for a in range(1, his):
        outward["loss", a] = push(
            loss_mid.at[around("hi", a)], loss_far.at[a], lf_s.at[a], lf_r.at[a], hi_peers[a - 1]
        )
    for a in order:
        total = grad[lo, around("hi", a)].astype(F32)
        for b in range(1, los):
            copies[b, a].wait_recv()
            total = total + near[b, a].astype(F32)
        if a > 0:
            mid[a] = total.astype(BF)
            outward[a] = push(mid.at[a], far.at[a], far_s.at[a], far_r.at[a], hi_peers[a - 1])
        else:
            sum_out[...] = total
    own_loss = loss_mid[hi]
    total = sum_out[...]
    for a in range(1, his):
        outward["loss", a].wait_recv()
        own_loss = own_loss + loss_far[a]
        outward[a].wait_recv()
        total = total + far[a].astype(F32)
    loss_out[...] = own_loss
    sum_out[...] = total
    sig = jax.nn.sigmoid(gates[1].astype(F32))
    own_gates[0] = (total * sig).astype(BF)
    own_gates[1] = (total * gates[0].astype(F32) * sig * (1.0 - sig)).astype(BF)
    spreads = [
        push(own_gates, all_gates.at[b], gate_s.at[b], gate_r.at[b], lo_peers[b - 1])
        for b in range(1, los)
    ]
    rows = lax.broadcasted_iota(jnp.int32, (local, reach), 0) % LEN
    conv_copy.wait()
    for b in range(los):
        if b > 0:
            spreads[b - 1].wait_recv()
            part = all_gates.at[b]
        else:
            part = own_gates
        wide = dot_t(part[0], conv[0]) + dot_t(part[1], conv[1])
        terms = wide[:, :reach]
        for tap in range(1, wide.shape[1] // reach):
            moved = pltpu.roll(wide[:, tap * reach : (tap + 1) * reach], local - tap, 0)
            terms = terms + jnp.where(rows < LEN - tap, moved, 0.0)
        terms_out[b] = terms.astype(BF)
        if b > 0:
            peer = device(lo=around("lo", -b))
            ends.append(
                push(terms_out.at[b], conv_out.at[lo], term_s.at[b], term_r.at[b], peer)
            )
        else:
            kept = pltpu.make_async_copy(terms_out.at[0], conv_out.at[lo], own)
            kept.start()
    for copy in list(copies.values()) + list(outward.values()) + spreads:
        copy.wait_send()
    for copy in ends:
        copy.wait()
    kept.wait()


def scatter(grad, gates, conv, loss):
    los, his, local, narrow = grad.shape
    halves, taps, reach, _ = conv.shape
    conv = conv.reshape(halves, taps * reach, narrow)
    loss = jnp.broadcast_to(loss.reshape(los, his, 1, local), (los, his, 8, local))
    dma = pltpu.SemaphoreType.DMA
    inside = pl.BlockSpec(memory_space=pltpu.VMEM)
    return pl.pallas_call(
        scatter_kernel,
        out_shape=(
            jax.ShapeDtypeStruct((local, narrow), F32),
            jax.ShapeDtypeStruct((los, local, reach), BF),
            jax.ShapeDtypeStruct((8, local), F32),
        ),
        in_specs=[inside, inside, pl.BlockSpec(memory_space=pl.ANY), inside],
        out_specs=(inside, pl.BlockSpec(memory_space=pl.ANY), inside),
        scratch_shapes=[
            pltpu.VMEM((los, his, local, narrow), BF),
            pltpu.VMEM((his, local, narrow), BF),
            pltpu.VMEM((his, local, narrow), BF),
            pltpu.VMEM(gates.shape, BF),
            pltpu.VMEM((los, *gates.shape), BF),
            pltpu.VMEM((los, local, reach), BF),
            pltpu.VMEM((los, his, 8, local), F32),
            pltpu.VMEM((his, 8, local), F32),
            pltpu.VMEM((his, 8, local), F32),
            dma((los, his)),
            dma((los, his)),
            dma((his,)),
            dma((his,)),
            dma((los,)),
            dma((los,)),
            dma((los,)),
            dma((los,)),
            dma((los,)),
            dma((los,)),
            dma((his,)),
            dma((his,)),
            dma,
            pltpu.VMEM(conv.shape, BF),
            dma,
        ],
        compiler_params=pltpu.CompilerParams(
            collective_id=1, has_side_effects=True, vmem_limit_bytes=32 << 20
        ),
    )(grad, gates, conv, loss)


def running_count(mine):
    local = mine.shape[1]
    upto = (jnp.arange(local)[:, None] <= jnp.arange(local)[None, :]).astype(F32)
    within = dot(mine, upto)
    blocks = mine.shape[0]
    before = (jnp.arange(blocks)[None, :] < jnp.arange(blocks)[:, None]).astype(F32)
    return within + dot(before, within[:, -1:])


def tier_start(rows, word_ids, proj, out_shard, ch_index):
    features = dot(rows, proj).astype(BF)
    logits = dot(features, out_shard)
    top = jnp.max(logits, axis=1)
    total = jnp.sum(jnp.exp(logits - top[:, None]), axis=1)
    width = out_shard.shape[1]
    positions = jnp.arange(width, dtype=jnp.int32) + ch_index * width
    hot = positions[None, :] == word_ids[:, None]
    picked = jnp.sum(jnp.where(hot, logits, 0.0), axis=1)
    return features, logits, hot, picked, jnp.stack([top, total])


def tier_slope(logits, hot, member, log_total):
    slope = jnp.exp(logits - log_total[:, None]) - hot.astype(F32)
    return jnp.where(member[:, None], slope, 0.0).astype(BF)


def on_device(
    hidden,
    pre_gates,
    conv_weight,
    head_weight,
    cluster_weight,
    tail1_proj,
    tail2_proj,
    tail1_out,
    tail2_out,
    cluster_id,
    target,
):
    local, model_width = hidden.shape
    owners = lax.axis_size(TOK)
    groups = lax.axis_size("ch")
    lo = lax.axis_size("lo")
    me = lax.axis_index(TOK)
    ch_index = lax.axis_index("ch")
    tokens = local * owners
    slots = max(2, local // owners) * owners
    narrow = model_width // groups
    col_start = ch_index * narrow

    def group_at(step):
        return lax.rem(ch_index + step + groups, groups) * narrow

    hidden_own = lax.dynamic_slice_in_dim(hidden, col_start, narrow, 1)
    clusters = cluster_weight.shape[1]
    share = cluster_weight.shape[0]
    ids = jnp.stack([cluster_id, target // 256, target % 256]).astype(BF)
    small = jnp.concatenate([cluster_weight.reshape(-1), ids.reshape(-1)])
    used = small.shape[0]
    small = jnp.pad(small, (0, -used % (16 * LANES))).reshape(-1, LANES)
    hidden_all, small, word_part = gather(hidden_own, small, head_weight)
    hidden_by_step = [hidden_all[step].reshape(tokens, narrow) for step in range(groups)]
    small = small.reshape(owners, -1)
    cluster_part = small[:, : share * clusters].reshape(model_width, clusters)
    ids = small[:, share * clusters : used].astype(jnp.int32).reshape(owners // lo, lo, 3, local)
    ids = ids.transpose(2, 1, 0, 3).reshape(3, tokens)
    cluster_all, target_all = ids[0], ids[1] * 256 + ids[2]

    words = head_weight.shape[1] // owners
    conv_weight, word_part = lax.optimization_barrier((conv_weight, word_part))
    conv_part = lax.all_gather(conv_weight, "hi", axis=2, tiled=True)

    mine = (cluster_all >= 0) & (cluster_all // 2 == me)
    rank = running_count(mine.reshape(owners, local).astype(F32)).reshape(tokens)
    slot_ids = jnp.where(mine, rank.astype(jnp.int32) - 1, -1)
    chosen = slot_ids[:, None] == jnp.arange(slots, dtype=jnp.int32)[None, :]
    chosen_bf = chosen.astype(BF)
    rows = jnp.zeros((slots, model_width), BF)
    for step, part in enumerate(hidden_by_step):
        picked_part = t_dot(chosen_bf, part).astype(BF)
        rows = lax.dynamic_update_slice_in_dim(rows, picked_part, group_at(-step), 1)
    word_ids = jnp.sum(jnp.where(chosen, target_all[:, None], 0), axis=0)
    tiers = jnp.sum(jnp.where(chosen, cluster_all[:, None] % 2 + 1, 0), axis=0)
    first_member, second_member = tiers == 1, tiers == 2
    first_proj, second_proj = tail1_proj[0], tail2_proj[0]
    first_out, second_out = tail1_out[0], tail2_out[0]
    first_features, first_logits, first_hot, first_pick, first_stats = tier_start(
        rows, word_ids, first_proj, first_out, ch_index
    )
    second_features, second_logits, second_hot, second_pick, second_stats = tier_start(
        rows, word_ids, second_proj, second_out, ch_index
    )
    stats = lax.all_gather(jnp.stack([first_stats, second_stats], axis=1), "ch")
    top, total = merge_stats(stats)
    tail_log = top + jnp.log(total)
    first_slope = tier_slope(first_logits, first_hot, first_member, tail_log[0])
    second_slope = tier_slope(second_logits, second_hot, second_member, tail_log[1])
    dz = jnp.concatenate(
        [dot_t(first_slope, first_out), dot_t(second_slope, second_out)], axis=1
    )
    dz = jnp.sum(lax.all_gather(dz, "ch"), axis=0).astype(BF)
    first_dz = dz[:, : first_proj.shape[1]]
    second_dz = dz[:, first_proj.shape[1] :]
    first_own = lax.dynamic_slice_in_dim(first_proj, col_start, narrow, 0)
    second_own = lax.dynamic_slice_in_dim(second_proj, col_start, narrow, 0)
    back = (dot_t(first_dz, first_own) + dot_t(second_dz, second_own)).astype(BF)
    once = jnp.where(ch_index == 0, 1.0, 0.0)
    tail_loss = jnp.where(first_member, once * tail_log[0] - first_pick, 0.0)
    tail_loss = tail_loss + jnp.where(second_member, once * tail_log[1] - second_pick, 0.0)
    first_out_grad = t_dot(first_features, first_slope)
    second_out_grad = t_dot(second_features, second_slope)
    rows_part = lax.dynamic_slice_in_dim(rows, col_start, narrow, 1)
    first_proj_grad = t_dot(rows_part, first_dz)
    second_proj_grad = t_dot(rows_part, second_dz)

    spare = -(words + clusters) % LANES
    columns = jnp.concatenate(
        [word_part, cluster_part, jnp.zeros((model_width, spare), BF)], axis=1
    )
    place = jnp.arange(columns.shape[1], dtype=jnp.int32)[None, :]
    limit = jnp.where(me == 0, words + clusters, words)
    logits = sum(
        dot(part, lax.dynamic_slice_in_dim(columns, group_at(-step), narrow, 0))
        for step, part in enumerate(hidden_by_step)
    )
    logits = jnp.where(place < limit, logits, -jnp.inf)
    top = jnp.max(logits, axis=1)
    total = jnp.sum(jnp.exp(logits - top[:, None]), axis=1)
    is_tail = cluster_all >= 0
    word_place = target_all - (ch_index * owners + me) * words
    word_place = jnp.where((word_place >= 0) & (word_place < words), word_place, -1)
    cluster_place = cluster_all - ch_index * clusters
    cluster_here = (cluster_place >= 0) & (cluster_place < clusters) & (me == 0)
    cluster_place = jnp.where(cluster_here, cluster_place + words, -1)
    hot = place == jnp.where(is_tail, cluster_place, word_place)[:, None]
    picked = jnp.sum(jnp.where(hot, logits, 0.0), axis=1)
    stats = lax.all_gather(jnp.stack([top, total]), "ch")
    stats = spread(jnp.stack(merge_stats(stats)), TOK)
    top, total = merge_stats(stats)
    head_log = top + jnp.log(total)
    slope = (jnp.exp(logits - head_log[:, None]) - hot.astype(F32)).astype(BF)
    grad_sum = 0.0
    for step in range(1, groups):
        block = lax.dynamic_slice_in_dim(columns, group_at(step), narrow, 0)
        grad_sum = grad_sum + turned(dot_t(slope, block).astype(BF), step).astype(F32)
    block = lax.dynamic_slice_in_dim(columns, col_start, narrow, 0)
    own_part = dot_t(
        jnp.concatenate([slope, chosen_bf], axis=1), jnp.concatenate([block, back.T], axis=1)
    )
    grad_sum = (grad_sum + own_part).astype(BF).reshape(lo, owners // lo, local, narrow)
    loss_part = jnp.sum(jnp.where(chosen, tail_loss[None, :], 0.0), axis=1) - picked
    grad_sum, conv_terms, own_loss = scatter(grad_sum, pre_gates, conv_part, loss_part)
    own_loss = jnp.sum(lax.all_gather(own_loss[0], "ch"), axis=0)
    own_log = lax.dynamic_index_in_dim(
        head_log.reshape(lo, owners // lo, local).transpose(1, 0, 2).reshape(owners, local),
        me,
        keepdims=False,
    )
    token_loss = own_loss + own_log

    conv_terms = conv_terms.reshape(lo, local, owners // lo, share).transpose(1, 2, 0, 3)
    conv_terms = conv_terms.reshape(local, model_width)
    conv_grad = lax.dynamic_slice_in_dim(conv_terms, col_start, narrow, 1).astype(F32)
    for step in range(1, groups):
        block = lax.dynamic_slice_in_dim(conv_terms, group_at(step), narrow, 1)
        conv_grad = conv_grad + turned(block, step).astype(F32)
    grad_input = (grad_sum + conv_grad).astype(BF)
    return (
        token_loss,
        grad_input,
        first_proj_grad[None],
        second_proj_grad[None],
        first_out_grad[None],
        second_out_grad[None],
    )


def solution(mesh):
    n_tok, n_ch = mesh.shape["tok"], mesh.shape["ch"]
    lo = 1
    while n_tok % (lo * 2) == 0 and lo * lo * 4 <= n_tok:
        lo *= 2
    split = Mesh(mesh.devices.reshape(n_tok // lo, lo, n_ch), ("hi", "lo", "ch"))
    placed = (
        P(TOK, None),
        P(None, TOK, "ch"),
        P(None, None, TOK, "ch"),
        P(TOK, "ch"),
        P(TOK, "ch"),
        P(TOK, None, None),
        P(TOK, None, None),
        P(TOK, None, "ch"),
        P(TOK, None, "ch"),
        P(TOK),
        P(TOK),
    )
    return jax.shard_map(
        on_device,
        mesh=split,
        in_specs=placed,
        out_specs=(
            P(TOK),
            P(TOK, "ch"),
            P(TOK, "ch", None),
            P(TOK, "ch", None),
            P(TOK, None, "ch"),
            P(TOK, None, "ch"),
        ),
        check_vma=False,
    )
```
